512 devices in a mesh: gx: 64 (over y_hi, z, core), gy: 8 (over y_lo, x).
Axes of the slice: x: 4, y: 8 (y_hi: 4, y_lo: 2; y = y_hi * 2 + y_lo), z: 8, core: 2. Of those that a mesh axis runs over, the one named last changes fastest.
Arguments:
- gas_state: float32 [5, 512, 64, 1024], P(None, 'gx', 'gy'), may hold values from -6 to 6
- mixing: float32 [512, 64, 1024], P('gx', 'gy'), may hold values from 0.02 to 0.15
- particles: float32 [8, 1048576], P(None, ('gx', 'gy')), as said below
- cell_index: int32 [1048576], P(('gx', 'gy')), may hold values from 0 to 65535
- size_class: int32 [1048576], P(('gx', 'gy')), may hold values from 0 to 6
- destination: int32 [1048576], P(('gx', 'gy')), may hold values from 0 to 8, as said below
- slot: int32 [1048576], P(('gx', 'gy')), may hold values from 0 to 127, as said below
- drag_rate: float32 [7], replicated, may hold values from 0.1 to 2
- settling: float32 [7], replicated, may hold values from 0.3 to 3
- heat_rate: float32 [7], replicated, may hold values from 0.05 to 1
Outputs:
- gas_next: float32 [5, 512, 64, 1024], P(None, 'gx', 'gy')
- kept: float32 [8, 1048576], P(None, ('gx', 'gy'))
- arrived: float32 [8, 8, 65536], P(None, None, ('gx', 'gy'))
The draws below stay inside these ranges and needn't reach their ends.
Inputs may be any that keep to these rules, and one draw needn't show every extreme that they name: Destinations 1 to 8 follow the order of the steps; each tile sends to every destination between 1 and 128 particles, and in every draw each tile sends exactly 128 to one destination. Moving particles of one tile with one destination take distinct slots 0 to count - 1; staying particles have slot 0. `particles`: attribute 7 (mass) lies in 0.25 to 2.
All inputs are finite; a program needn't handle non-finite values.
Results may differ from the reference program's by a relative error of at most 0.0001.
Values sent between devices are 32-bit elements; how exact they have to be, the bound alone decides.
A program may use at most 64 MiB of HBM per device.

```python
import math
import jax
import jax.numpy as jnp
import numpy as np

CX = 8
CY = 8
NZ = 1024
PDEV = 2048
NCLASS = 7
NCOMP = 5
NATTR = 8
CAP = 128
CELLS = 65536
NX = 512
NY = 64
PTOT = 1048576
CAPS = 65536
N_GX = 64
N_GY = 8


def routing(key):
    devices = PTOT // PDEV
    key_limit, key_count, key_force, key_perm = jax.random.split(key, 4)
    limits = jax.random.randint(key_limit, (devices, 1), CAP // 8 + 1, CAP + 1)
    counts = jax.random.randint(key_count, (devices, 8), 0, 1 << 20) % limits + 1
    forced = jax.random.randint(key_force, (devices, 1), 0, 8)
    counts = jnp.where(jnp.arange(8, dtype=jnp.int32)[None, :] == forced, CAP, counts)
    bounds = jnp.cumsum(counts, axis=1)
    position = jnp.arange(PDEV, dtype=jnp.int32)
    bucket = jnp.sum((position[None, :, None] >= bounds[:, None, :]).astype(jnp.int32), axis=2)
    starts = bounds - counts
    begin = jnp.take_along_axis(starts, jnp.minimum(bucket, 7), axis=1)
    target = jnp.where(bucket < 8, bucket + 1, 0)
    placed = jnp.where(bucket < 8, position[None, :] - begin, 0)
    subkeys = jax.random.split(key_perm, devices)

    def permute_one(subkey):
        return jax.random.permutation(subkey, PDEV)
    order = jax.vmap(permute_one)(subkeys)
    target = jnp.take_along_axis(target, order, axis=1)
    placed = jnp.take_along_axis(placed, order, axis=1)
    return (target.reshape(-1).astype(jnp.int32), placed.reshape(-1).astype(jnp.int32))


def draw_destination(key, part):
    return routing(jax.random.fold_in(key, 7))[0]


def draw_slot(key, part):
    return routing(jax.random.fold_in(key, 7))[1]


def draw_particles(key, part):
    key_base, key_mass = jax.random.split(jax.random.fold_in(key, 11))
    base = jax.random.normal(key_base, (NATTR, PTOT), jnp.float32)
    grain_bundle_weight = jnp.exp(jax.random.uniform(key_mass, (PTOT,), jnp.float32, math.log(0.25), math.log(2.0)))
    return base.at[7].set(grain_bundle_weight)


def with_ends(result, rng, smallest, high):
    shape = result.shape
    place = [jax.random.randint(jax.random.fold_in(rng, axis), (), 0, shape[axis]) for axis in range(len(shape))]
    result = result.at[tuple(place)].set(smallest)
    longest = shape.index(max(shape))
    place[longest] = (place[longest] + 1) % shape[longest]
    return result.at[tuple(place)].set(high)


def levels(own_key, extent, cuts, smallest, top_value):
    loudness = 1.0
    for dim, shards_of in cuts:
        heights = jax.random.uniform(jax.random.fold_in(jax.random.fold_in(own_key, 6), dim), (shards_of,), jnp.float32, smallest / len(cuts), top_value / len(cuts))
        loudness = loudness * jnp.repeat(jnp.exp(heights), extent[dim] // shards_of).reshape((-1,) + (1,) * (len(extent) - 1 - dim))
    return loudness


def normal_values(rng, shape, width, limit, cuts=(), kind=jnp.bfloat16):
    values = width * jax.random.normal(rng, shape, jnp.float32)
    if cuts:
        values = values * levels(rng, shape, cuts, -0.22, 0.18)
    return jnp.clip(values, -limit, limit).astype(kind)


def setup_inputs(seed: int = 0) -> dict:
    key_of = jax.random.split(jax.random.key(seed), 11)
    gas_state = normal_values(key_of[0], (NCOMP, NX, NY, NZ), 1.0, 6.0, ((1, 64), (2, 8)), jnp.float32)
    mixing = jnp.clip(0.02 + 0.13000001 * jax.random.uniform(key_of[1], (NX, NY, NZ), jnp.float32) ** levels(key_of[1], (NX, NY, NZ), ((0, 64), (1, 8)), -0.2, 0.2), 0.02, 0.15)
    particles = draw_particles(jax.random.fold_in(key_of[10], 71), 0)
    cell_index = with_ends(jax.random.randint(key_of[3], (PTOT,), 0, CELLS), jax.random.fold_in(key_of[3], 1), 0, CELLS - 1).astype(jnp.int32)
    size_class = with_ends(jax.random.randint(key_of[4], (PTOT,), 0, NCLASS), jax.random.fold_in(key_of[4], 1), 0, NCLASS - 1).astype(jnp.int32)
    destination = draw_destination(jax.random.fold_in(key_of[10], 71), 0)
    slot = draw_slot(jax.random.fold_in(key_of[10], 71), 0)
    drag_rate = jnp.clip(jnp.exp(jax.random.uniform(key_of[7], (NCLASS,), jnp.float32, math.log(0.1), math.log(2.0))), 0.1, 2.0)
    settling = jnp.clip(jnp.exp(jax.random.uniform(key_of[8], (NCLASS,), jnp.float32, math.log(0.3), math.log(3.0))), 0.3, 3.0)
    heat_rate = jnp.clip(jnp.exp(jax.random.uniform(key_of[9], (NCLASS,), jnp.float32, math.log(0.05), math.log(1.0))), 0.05, 1.0)
    return {"gas_state": gas_state, "mixing": mixing, "particles": particles, "cell_index": cell_index, "size_class": size_class, "destination": destination, "slot": slot, "drag_rate": drag_rate, "settling": settling, "heat_rate": heat_rate}


STEP_FIRST = np.array([0, -1, -1, -1, 0, 0, 1, 1, 1], dtype=np.int32)
STEP_SECOND = np.array([0, -1, 0, 1, -1, 1, -1, 0, 1], dtype=np.int32)


def particle_update(grain_descriptors, fluid_probed_state, drag, fall, thermal_transfer_flux):
    location = grain_descriptors[0:3]
    grain_motion_rate = grain_descriptors[3:6]
    grain_warmth_level = grain_descriptors[6]
    grain_bundle_weight = grain_descriptors[7]
    target = jnp.concatenate([fluid_probed_state[0:2], fluid_probed_state[2:3] - fall[None]], axis=0)
    motion_rate_following = (grain_motion_rate + drag[None] * target) / (1.0 + drag[None])
    warmth_following = (grain_warmth_level + thermal_transfer_flux * fluid_probed_state[3]) / (1.0 + thermal_transfer_flux)
    advanced_coordinates = location + motion_rate_following
    refreshed_result = jnp.concatenate([advanced_coordinates, motion_rate_following, warmth_following[None], grain_bundle_weight[None]], axis=0)
    coupling_return_force = jnp.concatenate([grain_bundle_weight[None] * (grain_motion_rate - motion_rate_following), (grain_bundle_weight * (grain_warmth_level - warmth_following))[None]], axis=0)
    return refreshed_result, coupling_return_force


def reference(gas_state, mixing, particles, cell_index, size_class, destination, slot, drag_rate, settling, heat_rate):
    tiles_first = N_GX
    tiles_second = N_GY
    tile_gas = gas_state.reshape(NCOMP, tiles_first, CX, tiles_second, CY, NZ).transpose(1, 3, 0, 2, 4, 5).reshape(tiles_first, tiles_second, NCOMP, CELLS)
    cells = cell_index.reshape(tiles_first, tiles_second, PDEV)
    fluid_probed_state = jnp.take_along_axis(tile_gas, cells[:, :, None, :], axis=3).transpose(2, 0, 1, 3)
    grain_descriptors = particles.reshape(NATTR, tiles_first, tiles_second, PDEV)
    drag = drag_rate[size_class].reshape(tiles_first, tiles_second, PDEV)
    fall = settling[size_class].reshape(tiles_first, tiles_second, PDEV)
    thermal_transfer_flux = heat_rate[size_class].reshape(tiles_first, tiles_second, PDEV)
    refreshed_result, coupling_return_force = particle_update(grain_descriptors, fluid_probed_state, drag, fall, thermal_transfer_flux)
    tile_number = jnp.arange(tiles_first * tiles_second, dtype=jnp.int32).reshape(tiles_first, tiles_second, 1)
    segment = (tile_number * CELLS + cells).astype(jnp.int32).reshape(-1)
    deposits = []
    for component in range(4):
        summed = jax.ops.segment_sum(coupling_return_force[component].reshape(-1), segment, num_segments=tiles_first * tiles_second * CELLS)
        summed = summed.reshape(tiles_first, tiles_second, CX, CY, NZ).transpose(0, 2, 1, 3, 4).reshape(NX, NY, NZ)
        deposits.append(summed)
    deposits.append(jnp.zeros((NX, NY, NZ), jnp.float32))
    deposit = jnp.stack(deposits)
    padded = jnp.pad(gas_state, ((0, 0), (1, 1), (1, 1), (1, 1)))
    beside = padded[:, 2:, 1:-1, 1:-1] + padded[:, :-2, 1:-1, 1:-1]
    beside = beside + padded[:, 1:-1, 2:, 1:-1] + padded[:, 1:-1, :-2, 1:-1]
    beside = beside + padded[:, 1:-1, 1:-1, 2:] + padded[:, 1:-1, 1:-1, :-2]
    gas_next = gas_state + mixing[None] * (beside - 6.0 * gas_state) + deposit
    dest = destination.reshape(tiles_first, tiles_second, PDEV)
    kept = jnp.where(dest[None] == 0, refreshed_result, 0.0).reshape(NATTR, PTOT)
    shift_first = jnp.asarray(STEP_FIRST)[dest].astype(jnp.float32)
    shift_second = jnp.asarray(STEP_SECOND)[dest].astype(jnp.float32)
    sent = jnp.concatenate([refreshed_result[0:1] - shift_first[None] * CX, refreshed_result[1:2] - shift_second[None] * CY, refreshed_result[2:]], axis=0)
    grid_first = jnp.broadcast_to(jnp.arange(tiles_first, dtype=jnp.int32)[:, None, None], dest.shape)
    grid_second = jnp.broadcast_to(jnp.arange(tiles_second, dtype=jnp.int32)[None, :, None], dest.shape)
    slots = slot.reshape(tiles_first, tiles_second, PDEV)
    buffers = jnp.zeros((tiles_first, tiles_second, 9, NATTR, CAP), jnp.float32)
    buffers = buffers.at[grid_first, grid_second, dest, :, slots].set(sent.transpose(1, 2, 3, 0))
    received = []
    for number in range(1, 9):
        step_first = int(STEP_FIRST[number])
        step_second = int(STEP_SECOND[number])
        source = jnp.pad(buffers[:, :, number], ((1, 1), (1, 1), (0, 0), (0, 0)))
        received.append(source[1 - step_first:1 - step_first + tiles_first, 1 - step_second:1 - step_second + tiles_second])
    arrived = jnp.stack(received).transpose(0, 3, 1, 2, 4).reshape(8, NATTR, CAPS)
    return gas_next, kept, arrived
```

```python
import functools

import jax
import jax.numpy as jnp
from jax import lax
from jax.experimental import pallas as pl
from jax.experimental.pallas import tpu as pltpu
from jax.sharding import PartitionSpec as P

MESH = pl.DeviceIdType.MESH
STEPS = ((-1, -1), (-1, 0), (-1, 1), (0, -1), (0, 1), (1, -1), (1, 0), (1, 1))
F32, BF16 = jnp.float32, jnp.bfloat16
BLOCK = 256
CHUNK = 256


def split2(x):
    hi = x.astype(BF16)
    return hi, (x - hi.astype(F32)).astype(BF16)


def kernel(
    remote,
    gas, mixing, grains, cell, kind, dest, slot, drag_h, settle_h, heat_h,
    out_v, kept_v, landing,
    gas_v, mix_v, grain_v, cell_v, kind_v, dest_v, slot_v,
    pieces, hot, fluid, weighted, edge_y, halo_x, halo_y, sending, drag_t, settle_t, heat_t,
    load_sem, send_sem, recv_sem,
):
    comps, si, sj, levels = gas.shape
    cols = si * sj
    slots = grains.shape[1]
    capacity = landing.shape[2]
    nx, ny = remote
    if nx > 1:
        ix, iy = lax.axis_index("gx"), lax.axis_index("gy")

        def at(dx, dy):
            return (lax.rem(ix + dx + nx, nx), lax.rem(iy + dy + ny, ny))

        barrier = pltpu.get_barrier_semaphore()
        for dx, dy in STEPS:
            pl.semaphore_signal(barrier, inc=1, device_id=at(dx, dy), device_id_type=MESH)

    loads = [
        pltpu.make_async_copy(src, dst, load_sem.at[n])
        for n, (src, dst) in enumerate(
            ((cell, cell_v), (gas, gas_v), (grains, grain_v), (kind, kind_v), (dest, dest_v), (slot, slot_v), (mixing, mix_v),
             (drag_h, drag_t), (settle_h, settle_t), (heat_h, heat_t))
        )
    ]
    for load in loads:
        load.start()

    loads[0].wait()
    for n in range(slots // BLOCK):
        span = slice(n * BLOCK, (n + 1) * BLOCK)
        level = cell_v[:, span] & (levels - 1)
        rows = lax.broadcasted_iota(jnp.int32, (levels, BLOCK), 0)
        hot[:, span] = jnp.where(rows == level, 1.0, 0.0).astype(BF16)

    copies = []
    if nx > 1:
        pl.semaphore_wait(barrier, len(STEPS))
        for side, (row, step) in enumerate(((si - 1, 1), (0, -1))):
            copies.append(
                pltpu.make_async_remote_copy(
                    gas.at[:, row], halo_x.at[side], send_sem.at[side], recv_sem.at[side], at(step, 0), MESH
                )
            )
            copies[-1].start()
    loads[1].wait()
    for side, (row, step) in enumerate(((sj - 1, 1), (0, -1))):
        for c in range(comps):
            edge_y[side, c] = gas_v[c, :, row, :]
        if nx > 1:
            copies.append(
                pltpu.make_async_remote_copy(
                    edge_y.at[side], halo_y.at[side], send_sem.at[2 + side], recv_sem.at[2 + side], at(0, step), MESH
                )
            )
            copies[-1].start()

    for c in range(4):
        hi, lo = split2(gas_v[c].reshape(cols, levels))
        pieces[c * cols : (c + 1) * cols, :] = hi
        pieces[(4 + c) * cols : (5 + c) * cols, :] = lo
    for n in range(slots // BLOCK):
        span = slice(n * BLOCK, (n + 1) * BLOCK)
        picked = jnp.dot(pieces[...], hot[:, span], preferred_element_type=F32)
        picked = picked[: 4 * cols] + picked[4 * cols :]
        column = cell_v[:, span] // levels
        mask = lax.broadcasted_iota(jnp.int32, (cols, BLOCK), 0) == column
        for c in range(4):
            fluid[c : c + 1, span] = jnp.sum(
                jnp.where(mask, picked[c * cols : (c + 1) * cols], 0.0), axis=0, keepdims=True
            )

    for load in loads[2:]:
        load.wait()
    kinds = kind_v[...]
    drag = jnp.zeros(kinds.shape, F32)
    fall = jnp.zeros(kinds.shape, F32)
    heat = jnp.zeros(kinds.shape, F32)
    for k in range(drag_t.shape[0]):
        drag = jnp.where(kinds == k, drag_t[k], drag)
        fall = jnp.where(kinds == k, settle_t[k], fall)
        heat = jnp.where(kinds == k, heat_t[k], heat)
    now = grain_v[...]
    row = lax.broadcasted_iota(jnp.int32, now.shape, 0)
    rate = jnp.where(row == 6, heat, drag)
    target = jnp.where(row == 6, fluid[3:4, :], fluid[2:3, :] - fall)
    target = jnp.where(row == 3, fluid[0:1, :], jnp.where(row == 4, fluid[1:2, :], target))
    after = (now + rate * target) / (1.0 + rate)
    moved = now + pltpu.roll(after, 5, 0)
    new = jnp.where(row < 3, moved, jnp.where(row == 7, now, after))
    force = now[7:8] * (now - after)
    dests = dest_v[...]
    kept_v[...] = jnp.where(dests == 0, new, 0.0)
    first = jnp.where(dests <= 3, -1.0, jnp.where(dests >= 6, 1.0, 0.0))
    second = jnp.where(
        (dests == 1) | (dests == 4) | (dests == 6), -1.0, jnp.where((dests == 3) | (dests == 5) | (dests == 8), 1.0, 0.0)
    )
    sent = new - jnp.where(row == 0, first * si, jnp.where(row == 1, second * sj, 0.0))

    s0 = sent.astype(BF16).astype(F32)
    s1 = (sent - s0).astype(BF16).astype(F32)
    s2 = sent - s0 - s1
    left = jnp.concatenate(
        [jnp.where(dests == d + 1, s, 0.0) for s in (s0, s1, s2) for d in range(8)], axis=0
    ).astype(BF16)
    slot_hot = jnp.where(
        lax.broadcasted_iota(jnp.int32, (capacity, slots), 0) == slot_v[...], 1.0, 0.0
    ).astype(BF16)
    packed = lax.dot_general(left, slot_hot, (((1,), (1,)), ((), ())), preferred_element_type=F32)
    sending[...] = (packed[:64] + packed[64:128] + packed[128:]).reshape(8, 8, capacity)
    if nx > 1:
        for d, (dx, dy) in enumerate(STEPS):
            copies.append(
                pltpu.make_async_remote_copy(
                    sending.at[d], landing.at[d], send_sem.at[4 + d], recv_sem.at[4 + d], at(dx, dy), MESH
                )
            )
            copies[-1].start()

    f0 = force.astype(BF16).astype(F32)
    f1 = force - f0
    column = cell_v[...] // levels
    mask = lax.broadcasted_iota(jnp.int32, (cols, slots), 0) == column
    for k, f in enumerate((f0, f1)):
        for c in range(4):
            weighted[(4 * k + c) * cols : (4 * k + c + 1) * cols, :] = jnp.where(mask, f[3 + c : 4 + c], 0.0).astype(BF16)

    for copy in copies[:4]:
        copy.wait()
    for side in range(2):
        if nx > 1:
            outside_x = ix == (0 if side == 0 else nx - 1)
            outside_y = iy == (0 if side == 0 else ny - 1)
            halo_x[side] = jnp.where(outside_x, 0.0, halo_x[side])
            halo_y[side] = jnp.where(outside_y, 0.0, halo_y[side])

    wide = CHUNK + 256
    for n in range(levels // CHUNK):
        lo, hi = n * CHUNK, (n + 1) * CHUNK
        dep = lax.dot_general(
            weighted[...], hot[lo:hi, :], (((1,), (1,)), ((), ())), preferred_element_type=F32
        )
        dep = (dep[: 4 * cols] + dep[4 * cols :]).reshape(4, si, sj, CHUNK)
        jrow = lax.broadcasted_iota(jnp.int32, (sj, CHUNK), 0)
        lane = lax.broadcasted_iota(jnp.int32, (sj, CHUNK), 1)
        for c in range(comps):
            for i in range(si):
                here = gas_v[c, i, :, lo:hi]
                before = halo_x[0, c, :, lo:hi] if i == 0 else gas_v[c, i - 1, :, lo:hi]
                behind = halo_x[1, c, :, lo:hi] if i == si - 1 else gas_v[c, i + 1, :, lo:hi]
                left_j = jnp.where(jrow == 0, halo_y[0, c, i : i + 1, lo:hi], pltpu.roll(here, 1, 0))
                right_j = jnp.where(jrow == sj - 1, halo_y[1, c, i : i + 1, lo:hi], pltpu.roll(here, sj - 1, 0))
                below = gas_v[c, i, :, lo - 128 : lo] if lo > 0 else None
                above = gas_v[c, i, :, hi : hi + 128] if hi < levels else None
                zeros = jnp.zeros((sj, 128), F32)
                full = jnp.concatenate([zeros if below is None else below, here, zeros if above is None else above], axis=1)
                down = pltpu.roll(full, 1, 1)[:, 128 : 128 + CHUNK]
                up = pltpu.roll(full, wide - 1, 1)[:, 128 : 128 + CHUNK]
                beside = before + behind + left_j + right_j + down + up
                value = here + mix_v[i, :, lo:hi] * (beside - 6.0 * here)
                if c < 4:
                    value = value + dep[c, i]
                out_v[c, i, :, lo:hi] = value

    for copy in copies[4:]:
        copy.wait()
    if nx > 1:
        for d, (dx, dy) in enumerate(STEPS):
            from_x, from_y = ix - dx, iy - dy
            outside = (from_x < 0) | (from_x >= nx) | (from_y < 0) | (from_y >= ny)
            landing[d] = jnp.where(outside, 0.0, landing[d])
    else:
        landing[...] = sending[...]


def write_out(a, b, c, out_a, out_b, out_c, sems):
    copies = [
        pltpu.make_async_copy(src, dst, sems.at[n]) for n, (src, dst) in enumerate(((a, out_a), (b, out_b), (c, out_c)))
    ]
    for copy in copies:
        copy.start()
    for copy in copies:
        copy.wait()


def on_device(remote, gas, mixing, grains, cell, kind, dest, slot, drag, settle, heat):
    comps, si, sj, levels = gas.shape
    attrs, slots = grains.shape
    capacity = slots // 16
    row = (1, slots)
    hbm = pl.BlockSpec(memory_space=pltpu.HBM)
    vmem = pl.BlockSpec(memory_space=pltpu.VMEM)
    held = tuple(pltpu.with_memory_space_constraint(x, pltpu.HBM) for x in (
        gas, mixing, grains, cell.reshape(row), kind.reshape(row), dest.reshape(row), slot.reshape(row), drag, settle, heat))
    results = pl.pallas_call(
        functools.partial(kernel, remote),
        out_shape=(
            pltpu.VMEM(gas.shape, F32),
            pltpu.VMEM(grains.shape, F32),
            pltpu.VMEM((8, attrs, capacity), F32),
        ),
        in_specs=[hbm] * 10,
        out_specs=(vmem,) * 3,
        scratch_shapes=[
            pltpu.VMEM(gas.shape, F32),
            pltpu.VMEM(mixing.shape, F32),
            pltpu.VMEM(grains.shape, F32),
            pltpu.VMEM(row, jnp.int32),
            pltpu.VMEM(row, jnp.int32),
            pltpu.VMEM(row, jnp.int32),
            pltpu.VMEM(row, jnp.int32),
            pltpu.VMEM((8 * si * sj, levels), BF16),
            pltpu.VMEM((levels, slots), BF16),
            pltpu.VMEM((8, slots), F32),
            pltpu.VMEM((8 * si * sj, slots), BF16),
            pltpu.VMEM((2, comps, si, levels), F32),
            pltpu.VMEM((2, comps, sj, levels), F32),
            pltpu.VMEM((2, comps, si, levels), F32),
            pltpu.VMEM((8, attrs, capacity), F32),
            pltpu.SMEM(drag.shape, F32),
            pltpu.SMEM(settle.shape, F32),
            pltpu.SMEM(heat.shape, F32),
            pltpu.SemaphoreType.DMA((10,)),
            pltpu.SemaphoreType.DMA((12,)),
            pltpu.SemaphoreType.DMA((12,)),
        ],
        compiler_params=pltpu.CompilerParams(
            collective_id=0 if remote[0] > 1 else None,
            has_side_effects=True,
            vmem_limit_bytes=40 * 1024 * 1024,
        ),
        name="ash_step",
    )(*held)
    shapes = tuple(jax.ShapeDtypeStruct(r.shape, F32) for r in results)
    results = tuple(pltpu.with_memory_space_constraint(r, pltpu.VMEM) for r in results)
    return pl.pallas_call(
        write_out,
        out_shape=shapes,
        in_specs=[vmem] * 3,
        out_specs=(hbm,) * 3,
        scratch_shapes=[pltpu.SemaphoreType.DMA((3,))],
        name="write_out",
    )(*results)


def solution(mesh):
    tiles = P(None, ("gx", "gy"))
    per_slot = P(("gx", "gy"))
    return jax.shard_map(
        functools.partial(on_device, (mesh.shape["gx"], mesh.shape["gy"])),
        mesh=mesh,
        in_specs=(P(None, "gx", "gy", None), P("gx", "gy", None), tiles) + (per_slot,) * 4 + (P(),) * 3,
        out_specs=(P(None, "gx", "gy", None), tiles, P(None, None, ("gx", "gy"))),
        check_vma=False,
    )
```

```python
import functools

import jax
import jax.numpy as jnp
from jax import lax
from jax.experimental import pallas as pl
from jax.experimental.pallas import tpu as pltpu
from jax.sharding import PartitionSpec as P

MESH = pl.DeviceIdType.MESH
STEPS = ((-1, -1), (-1, 0), (-1, 1), (0, -1), (0, 1), (1, -1), (1, 0), (1, 1))
F32, BF16, I32 = jnp.float32, jnp.bfloat16, jnp.int32
BLOCK = 256
CHUNK = 256
RUN = 16
NT = (((1,), (1,)), ((), ()))


def split2(x):
    hi = x.astype(BF16)
    return hi, (x - hi.astype(F32)).astype(BF16)


def split3(x):
    first = x.astype(BF16).astype(F32)
    second = (x - first).astype(BF16).astype(F32)
    return first, second, x - first - second


def one_hot(rows, ids):
    return jnp.where(lax.broadcasted_iota(I32, (rows, ids.shape[1]), 0) == ids, 1.0, 0.0).astype(BF16)


def sampled(pieces, hot, column, cols):
    picked = jnp.dot(pieces[...], hot, preferred_element_type=F32)
    picked = picked[: 4 * cols] + picked[4 * cols :]
    mask = lax.broadcasted_iota(I32, (cols, column.shape[1]), 0) == column
    return [
        jnp.sum(jnp.where(mask, picked[c * cols : (c + 1) * cols], 0.0), axis=0, keepdims=True) for c in range(4)
    ]


def updated(now, kinds, fluid, drag_t, settle_t, heat_t):
    drag = jnp.zeros(kinds.shape, F32)
    fall = jnp.zeros(kinds.shape, F32)
    heat = jnp.zeros(kinds.shape, F32)
    for k in range(drag_t.shape[0]):
        drag = jnp.where(kinds == k, drag_t[k], drag)
        fall = jnp.where(kinds == k, settle_t[k], fall)
        heat = jnp.where(kinds == k, heat_t[k], heat)
    row = lax.broadcasted_iota(I32, now.shape, 0)
    rate = jnp.where(row == 6, heat, drag)
    target = jnp.where(row == 6, fluid[3], fluid[2] - fall)
    target = jnp.where(row == 3, fluid[0], jnp.where(row == 4, fluid[1], target))
    after = (now + rate * target) / (1.0 + rate)
    moved = now + pltpu.roll(after, 5, 0)
    new = jnp.where(row < 3, moved, jnp.where(row == 7, now, after))
    return after, new, row


def kernel(
    tiles,
    gas, mixing, grains, cell, kind, dest, slot, drag_h, settle_h, heat_h,
    out_v, kept_v, landing,
    gas_v, mix_v, grain_v, cell_v, kind_v, dest_v, slot_v, drag_t, settle_t, heat_t,
    pieces, hot, fluid, weighted, edge_y, halo_x, halo_y, sending,
    load_sem, send_sem, recv_sem,
):
    comps, si, sj, levels = gas.shape
    cols = si * sj
    slots = grains.shape[1]
    capacity = landing.shape[2]
    nx, ny = tiles
    remote = nx > 1

    if remote:
        ix, iy = lax.axis_index("gx"), lax.axis_index("gy")
        place = lax.rem(ix, RUN)
        early = (place == 0) & (ix > 0)
        late = jnp.logical_not(early)
        last = (place == RUN - 1) & (ix < nx - 1)
        slow = place >= RUN - 2

        def at(step):
            return (lax.rem(ix + step[0] + nx, nx), lax.rem(iy + step[1] + ny, ny))

        def inside(step):
            x, y = ix + step[0], iy + step[1]
            return (x >= 0) & (x < nx) & (y >= 0) & (y < ny)

        def number(flag):
            return flag.astype(I32)

        barrier = pltpu.get_barrier_semaphore()

        def greet(steps, when):
            for step in steps:
                @pl.when(when(step) & inside(step))
                def _():
                    pl.semaphore_signal(barrier, inc=1, device_id=at(step), device_id_type=MESH)

        high = 1 + number(iy > 0) + number(iy < ny - 1)
        greet(STEPS, lambda step: (place + step[0] >= 0) & (place + step[0] < RUN))

    def copy_of(n, src, dst, step):
        return pltpu.make_async_remote_copy(src, dst, send_sem.at[n], recv_sem.at[n], at(step), MESH)

    def halo_copy(n):
        if n < 2:
            side, row = n, (si - 1, 0)[n]
            return copy_of(n, gas.at[:, row], halo_x.at[side], ((1, 0), (-1, 0))[side])
        return copy_of(n, edge_y.at[n - 2], halo_y.at[n - 2], ((0, 1), (0, -1))[n - 2])

    halo_steps = ((1, 0), (-1, 0), (0, 1), (0, -1))

    def grain_copy(d):
        return copy_of(4 + d, sending.at[d], landing.at[d], STEPS[d])

    def send(copy, step, when):
        @pl.when(when & inside(step))
        def _():
            copy.start()

    loads = [
        pltpu.make_async_copy(src, dst, load_sem.at[n])
        for n, (src, dst) in enumerate(
            (
                (grains, grain_v), (cell, cell_v), (kind, kind_v), (dest, dest_v), (slot, slot_v),
                (drag_h, drag_t), (settle_h, settle_t), (heat_h, heat_t),
                (gas.at[0:4], gas_v.at[0:4]), (gas.at[4:5], gas_v.at[4:5]), (mixing, mix_v),
            )
        )
    ]
    for load in loads:
        load.start()

    if remote:
        wide = 1 + number(place > 0) + number(place < RUN - 1) + number(last)
        pl.semaphore_wait(barrier, wide * high - 1)
        send(halo_copy(0), halo_steps[0], True)
        greet(STEPS[:3], lambda step: early)
        greet(STEPS[5:], lambda step: last)
        send(halo_copy(1), halo_steps[1], late)

    for load in loads[:8]:
        load.wait()
    now, kinds, dests, cells = grain_v[...], kind_v[...], dest_v[...], cell_v[...]
    level, column = cells & (levels - 1), cells // levels
    slot_hot = one_hot(capacity, slot_v[...])
    ids = jnp.concatenate(
        [(level & -4), (level & 3), column, kinds + 1, jnp.zeros((4, slots), I32)], axis=0
    ).astype(F32)
    values = split3(now) + (ids,)
    left = jnp.concatenate(
        [jnp.where(dests == d, v, 0.0) for d in (6, 7, 8) for v in values], axis=0
    ).astype(BF16)
    ahead = lax.dot_general(left, slot_hot, NT, preferred_element_type=F32)
    ahead = jnp.concatenate([ahead[32 * d : 32 * (d + 1)] for d in range(3)], axis=1)
    ahead_now = ahead[0:8] + ahead[8:16] + ahead[16:24]
    ahead_ids = ahead[24:32].astype(I32)
    ahead_level = ahead_ids[0:1] + ahead_ids[1:2]
    ahead_hot = one_hot(levels, ahead_level)
    loads[8].wait()
    for c in range(4):
        hi, lo = split2(gas_v[c].reshape(cols, levels))
        pieces[c * cols : (c + 1) * cols, :] = hi
        pieces[(4 + c) * cols : (5 + c) * cols, :] = lo
    ahead_fluid = sampled(pieces, ahead_hot, ahead_ids[2:3], cols)
    _, ahead_new, ahead_row = updated(ahead_now, ahead_ids[3:4] - 1, ahead_fluid, drag_t, settle_t, heat_t)
    ahead_new = jnp.where(ahead_ids[3:4] > 0, ahead_new, 0.0)
    for d in range(5, 8):
        dx, dy = STEPS[d]
        span = slice((d - 5) * capacity, (d - 4) * capacity)
        filled, row = ahead_ids[3:4, span] > 0, ahead_row[:, span]
        shift = jnp.where(row == 0, float(dx * si), jnp.where(row == 1, float(dy * sj), 0.0))
        sending[d] = jnp.where(filled, ahead_new[:, span] - shift, 0.0)
        if remote:
            send(grain_copy(d), STEPS[d], True)

    loads[9].wait()
    for side, row in enumerate((sj - 1, 0)):
        for c in range(comps):
            edge_y[side, c] = gas_v[c, :, row, :]
        if remote:
            send(halo_copy(2 + side), halo_steps[2 + side], jnp.logical_not(slow))

    for n in range(slots // BLOCK):
        span = slice(n * BLOCK, (n + 1) * BLOCK)
        block_hot = one_hot(levels, cell_v[:, span] & (levels - 1))
        hot[:, span] = block_hot
        block_fluid = sampled(pieces, block_hot, cell_v[:, span] // levels, cols)
        for c in range(4):
            fluid[c : c + 1, span] = block_fluid[c]

    after, new, row = updated(now, kinds, [fluid[c : c + 1, :] for c in range(4)], drag_t, settle_t, heat_t)
    force = now[7:8] * (now - after)
    kept_v[...] = jnp.where(dests == 0, new, 0.0)
    first = jnp.where(dests <= 3, -1.0, 0.0)
    second = jnp.where((dests == 1) | (dests == 4), -1.0, jnp.where((dests == 3) | (dests == 5), 1.0, 0.0))
    sent = new - jnp.where(row == 0, first * si, jnp.where(row == 1, second * sj, 0.0))

    left = jnp.concatenate(
        [jnp.where(dests == d, s, 0.0) for s in split3(sent) for d in range(1, 6)] + [jnp.zeros((8, slots), F32)], axis=0
    ).astype(BF16)
    packed = lax.dot_general(left, slot_hot, NT, preferred_element_type=F32)
    packed = packed[:40] + packed[40:80] + packed[80:120]
    for d in range(5):
        sending[d] = packed[8 * d : 8 * (d + 1)]
        if remote:
            send(grain_copy(d), STEPS[d], late if d < 3 else True)
    if remote:
        for n in (2, 3):
            send(halo_copy(n), halo_steps[n], slow)

    f0 = force.astype(BF16).astype(F32)
    mask = lax.broadcasted_iota(I32, (cols, slots), 0) == column
    for k, f in enumerate((f0, force - f0)):
        for c in range(4):
            weighted[(4 * k + c) * cols : (4 * k + c + 1) * cols, :] = jnp.where(mask, f[3 + c : 4 + c], 0.0).astype(BF16)

    loads[10].wait()
    wide = CHUNK + 256
    for n in range(levels // CHUNK):
        lo, hi = n * CHUNK, (n + 1) * CHUNK
        dep = lax.dot_general(weighted[...], hot[lo:hi, :], NT, preferred_element_type=F32)
        dep = (dep[: 4 * cols] + dep[4 * cols :]).reshape(4, si, sj, CHUNK)
        jrow = lax.broadcasted_iota(I32, (sj, CHUNK), 0)
        zeros = jnp.zeros((sj, 128), F32)
        for c in range(comps):
            for i in range(si):
                here = gas_v[c, i, :, lo:hi]
                beside = jnp.where(jrow == 0, 0.0, pltpu.roll(here, 1, 0))
                beside = beside + jnp.where(jrow == sj - 1, 0.0, pltpu.roll(here, sj - 1, 0))
                if i > 0:
                    beside = beside + gas_v[c, i - 1, :, lo:hi]
                if i < si - 1:
                    beside = beside + gas_v[c, i + 1, :, lo:hi]
                below = gas_v[c, i, :, lo - 128 : lo] if lo > 0 else zeros
                above = gas_v[c, i, :, hi : hi + 128] if hi < levels else zeros
                full = jnp.concatenate([below, here, above], axis=1)
                beside = beside + pltpu.roll(full, 1, 1)[:, 128 : 128 + CHUNK]
                beside = beside + pltpu.roll(full, wide - 1, 1)[:, 128 : 128 + CHUNK]
                value = here + mix_v[i, :, lo:hi] * (beside - 6.0 * here)
                if c < 4:
                    value = value + dep[c, i]
                out_v[c, i, :, lo:hi] = value

    if not remote:
        landing[...] = sending[...]
        return

    @pl.when(early)
    def _():
        pl.semaphore_wait(barrier, high)
    send(halo_copy(1), halo_steps[1], early)
    for d in range(3):
        send(grain_copy(d), STEPS[d], early)

    def back(step):
        return (-step[0], -step[1])

    for n in (2, 3):
        @pl.when(inside(back(halo_steps[n])))
        def _():
            halo_copy(n).wait_recv()
            j = (0, sj - 1)[n - 2]
            for c in range(comps):
                for i in range(si):
                    out_v[c, i, j : j + 1, :] = (
                        out_v[c, i, j : j + 1, :] + mix_v[i, j : j + 1, :] * halo_y[n - 2, c, i : i + 1, :]
                    )
    for n in (1, 0):
        @pl.when(inside(back(halo_steps[n])))
        def _():
            halo_copy(n).wait_recv()
            i = (0, si - 1)[n]
            for c in range(comps):
                out_v[c, i] = out_v[c, i] + mix_v[i] * halo_x[n, c]
    for d in range(8):
        came = inside(back(STEPS[d]))

        @pl.when(came)
        def _():
            grain_copy(d).wait_recv()

        @pl.when(jnp.logical_not(came))
        def _():
            landing[d] = jnp.zeros(landing.shape[1:], F32)
    for n in range(4):
        @pl.when(inside(halo_steps[n]))
        def _():
            halo_copy(n).wait_send()
    for d in range(8):
        @pl.when(inside(STEPS[d]))
        def _():
            grain_copy(d).wait_send()


def write_out(a, b, c, out_a, out_b, out_c, sems):
    copies = [
        pltpu.make_async_copy(src, dst, sems.at[n]) for n, (src, dst) in enumerate(((a, out_a), (b, out_b), (c, out_c)))
    ]
    for copy in copies:
        copy.start()
    for copy in copies:
        copy.wait()


def on_device(tiles, gas, mixing, grains, cell, kind, dest, slot, drag, settle, heat):
    comps, si, sj, levels = gas.shape
    attrs, slots = grains.shape
    capacity = slots // 16
    row = (1, slots)
    hbm = pl.BlockSpec(memory_space=pltpu.HBM)
    vmem = pl.BlockSpec(memory_space=pltpu.VMEM)
    held = (gas, mixing, grains, cell.reshape(row), kind.reshape(row), dest.reshape(row), slot.reshape(row), drag, settle, heat)
    held = tuple(pltpu.with_memory_space_constraint(x, pltpu.HBM) for x in held)
    results = pl.pallas_call(
        functools.partial(kernel, tiles),
        out_shape=(
            pltpu.VMEM(gas.shape, F32),
            pltpu.VMEM(grains.shape, F32),
            pltpu.VMEM((8, attrs, capacity), F32),
        ),
        in_specs=[hbm] * 10,
        out_specs=(vmem,) * 3,
        scratch_shapes=[
            pltpu.VMEM(gas.shape, F32),
            pltpu.VMEM(mixing.shape, F32),
            pltpu.VMEM(grains.shape, F32),
            pltpu.VMEM(row, I32),
            pltpu.VMEM(row, I32),
            pltpu.VMEM(row, I32),
            pltpu.VMEM(row, I32),
            pltpu.SMEM(drag.shape, F32),
            pltpu.SMEM(settle.shape, F32),
            pltpu.SMEM(heat.shape, F32),
            pltpu.VMEM((8 * si * sj, levels), BF16),
            pltpu.VMEM((levels, slots), BF16),
            pltpu.VMEM((8, slots), F32),
            pltpu.VMEM((8 * si * sj, slots), BF16),
            pltpu.VMEM((2, comps, si, levels), F32),
            pltpu.VMEM((2, comps, sj, levels), F32),
            pltpu.VMEM((2, comps, si, levels), F32),
            pltpu.VMEM((8, attrs, capacity), F32),
            pltpu.SemaphoreType.DMA((11,)),
            pltpu.SemaphoreType.DMA((12,)),
            pltpu.SemaphoreType.DMA((12,)),
        ],
        compiler_params=pltpu.CompilerParams(
            collective_id=0 if tiles[0] > 1 else None,
            has_side_effects=True,
            vmem_limit_bytes=40 * 1024 * 1024,
        ),
        name="ash_step",
    )(*held)
    shapes = tuple(jax.ShapeDtypeStruct(r.shape, F32) for r in results)
    results = tuple(pltpu.with_memory_space_constraint(r, pltpu.VMEM) for r in results)
    return pl.pallas_call(
        write_out,
        out_shape=shapes,
        in_specs=[vmem] * 3,
        out_specs=(hbm,) * 3,
        scratch_shapes=[pltpu.SemaphoreType.DMA((3,))],
        name="write_out",
    )(*results)


def solution(mesh):
    tiles = P(None, ("gx", "gy"))
    per_slot = P(("gx", "gy"))
    return jax.shard_map(
        functools.partial(on_device, (mesh.shape["gx"], mesh.shape["gy"])),
        mesh=mesh,
        in_specs=(P(None, "gx", "gy", None), P("gx", "gy", None), tiles) + (per_slot,) * 4 + (P(),) * 3,
        out_specs=(P(None, "gx", "gy", None), tiles, P(None, None, ("gx", "gy"))),
        check_vma=False,
    )
```

```python
import functools

import jax
import jax.numpy as jnp
from jax import lax
from jax.experimental import pallas as pl
from jax.experimental.pallas import tpu as pltpu
from jax.sharding import PartitionSpec as P

MESH = pl.DeviceIdType.MESH
STEPS = ((-1, -1), (-1, 0), (-1, 1), (0, -1), (0, 1), (1, -1), (1, 0), (1, 1))
F32, BF16, I32 = jnp.float32, jnp.bfloat16, jnp.int32
BLOCK = 256
CHUNK = 256
RUN = 16
NT = (((1,), (1,)), ((), ()))


def split2(x):
    hi = x.astype(BF16)
    return hi, (x - hi.astype(F32)).astype(BF16)


def split3(x):
    first = x.astype(BF16).astype(F32)
    second = (x - first).astype(BF16).astype(F32)
    return first, second, x - first - second


def one_hot(rows, ids):
    return jnp.where(lax.broadcasted_iota(I32, (rows, ids.shape[1]), 0) == ids, 1.0, 0.0).astype(BF16)


def sampled(pieces, hot, column, cols):
    picked = jnp.dot(pieces[...], hot, preferred_element_type=F32)
    picked = picked[: 4 * cols] + picked[4 * cols :]
    mask = lax.broadcasted_iota(I32, (cols, column.shape[1]), 0) == column
    return [
        jnp.sum(jnp.where(mask, picked[c * cols : (c + 1) * cols], 0.0), axis=0, keepdims=True) for c in range(4)
    ]


def updated(now, kinds, fluid, drag_t, settle_t, heat_t):
    drag = jnp.zeros(kinds.shape, F32)
    fall = jnp.zeros(kinds.shape, F32)
    heat = jnp.zeros(kinds.shape, F32)
    for k in range(drag_t.shape[0]):
        drag = jnp.where(kinds == k, drag_t[k], drag)
        fall = jnp.where(kinds == k, settle_t[k], fall)
        heat = jnp.where(kinds == k, heat_t[k], heat)
    row = lax.broadcasted_iota(I32, now.shape, 0)
    rate = jnp.where(row == 6, heat, drag)
    target = jnp.where(row == 6, fluid[3], fluid[2] - fall)
    target = jnp.where(row == 3, fluid[0], jnp.where(row == 4, fluid[1], target))
    after = (now + rate * target) / (1.0 + rate)
    moved = now + pltpu.roll(after, 5, 0)
    new = jnp.where(row < 3, moved, jnp.where(row == 7, now, after))
    return after, new, row


def kernel(
    tiles,
    gas, mixing, grains, cell, kind, dest, slot, drag_h, settle_h, heat_h,
    out_v, kept_v, landing,
    gas_v, mix_v, grain_v, cell_v, kind_v, dest_v, slot_v, drag_t, settle_t, heat_t,
    pieces, hot, fluid, weighted, edge_y, halo_x, halo_y, sending,
    load_sem, send_sem, recv_sem, reply_sem, answer_sem,
):
    comps, si, sj, levels = gas.shape
    cols = si * sj
    slots = grains.shape[1]
    capacity = landing.shape[2]
    nx, ny = tiles
    remote = nx > 1

    if remote:
        ix, iy = lax.axis_index("gx"), lax.axis_index("gy")
        place = lax.rem(ix, RUN)
        follows = ix < (nx // RUN - 1) * RUN
        early = (place == 0) & (ix > 0)
        late = jnp.logical_not(early)
        last = (place == RUN - 1) & follows
        usual = jnp.logical_not(last)
        slow = place >= RUN - 2

        def at(step):
            return (lax.rem(ix + step[0] + nx, nx), lax.rem(iy + step[1] + ny, ny))

        def inside(step):
            x, y = ix + step[0], iy + step[1]
            return (x >= 0) & (x < nx) & (y >= 0) & (y < ny)

        def number(flag):
            return flag.astype(I32)

        barrier = pltpu.get_barrier_semaphore()

        def greet(steps, when, semaphore):
            for n, step in enumerate(steps):
                @pl.when(when(step) & inside(step))
                def _():
                    pl.semaphore_signal(semaphore(n), inc=1, device_id=at(step), device_id_type=MESH)

        def first_round(step):
            target = place + step[0]
            return usual & (target >= 0) & (target < jnp.where(follows, RUN - 1, RUN)) | (early & (step[0] < 0))

        high = 1 + number(iy > 0) + number(iy < ny - 1)
        greet(STEPS, first_round, lambda n: barrier)

    def copy_of(n, src, dst, step):
        return pltpu.make_async_remote_copy(src, dst, send_sem.at[n], recv_sem.at[n], at(step), MESH)

    def halo_copy(n):
        if n < 2:
            side, row = n, (si - 1, 0)[n]
            return copy_of(n, gas.at[:, row], halo_x.at[side], ((1, 0), (-1, 0))[side])
        return copy_of(n, edge_y.at[n - 2], halo_y.at[n - 2], ((0, 1), (0, -1))[n - 2])

    halo_steps = ((1, 0), (-1, 0), (0, 1), (0, -1))

    def grain_copy(d):
        return copy_of(4 + d, sending.at[d], landing.at[d], STEPS[d])

    def send(copy, step, when):
        @pl.when(when & inside(step))
        def _():
            copy.start()

    loads = [
        pltpu.make_async_copy(src, dst, load_sem.at[n])
        for n, (src, dst) in enumerate(
            (
                (grains, grain_v), (cell, cell_v), (kind, kind_v), (dest, dest_v), (slot, slot_v),
                (drag_h, drag_t), (settle_h, settle_t), (heat_h, heat_t),
                (gas.at[0:4], gas_v.at[0:4]), (gas.at[4:5], gas_v.at[4:5]), (mixing, mix_v),
            )
        )
    ]
    for load in loads:
        load.start()

    if remote:
        wide = 1 + number(place > 0) + number(place < RUN - 1)
        pl.semaphore_wait(barrier, jnp.where(last, high, wide * high - 1))
        send(halo_copy(0), halo_steps[0], True)
        greet(STEPS[5:], lambda step: last, lambda n: reply_sem.at[n])
        greet(STEPS[:3], lambda step: last, lambda n: barrier)
        greet(STEPS[5:], lambda step: (place == RUN - 2) & follows, lambda n: answer_sem)
        send(halo_copy(1), halo_steps[1], late & usual)

    for load in loads[:8]:
        load.wait()
    now, kinds, dests, cells = grain_v[...], kind_v[...], dest_v[...], cell_v[...]
    level, column = cells & (levels - 1), cells // levels
    slot_hot = one_hot(capacity, slot_v[...])
    ids = jnp.concatenate(
        [(level & -4), (level & 3), column, kinds + 1, jnp.zeros((4, slots), I32)], axis=0
    ).astype(F32)
    values = split3(now) + (ids,)
    left = jnp.concatenate(
        [jnp.where(dests == d, v, 0.0) for d in (6, 7, 8) for v in values], axis=0
    ).astype(BF16)
    ahead = lax.dot_general(left, slot_hot, NT, preferred_element_type=F32)
    ahead = jnp.concatenate([ahead[32 * d : 32 * (d + 1)] for d in range(3)], axis=1)
    ahead_now = ahead[0:8] + ahead[8:16] + ahead[16:24]
    ahead_ids = ahead[24:32].astype(I32)
    ahead_level = ahead_ids[0:1] + ahead_ids[1:2]
    ahead_hot = one_hot(levels, ahead_level)
    loads[8].wait()
    for c in range(4):
        hi, lo = split2(gas_v[c].reshape(cols, levels))
        pieces[c * cols : (c + 1) * cols, :] = hi
        pieces[(4 + c) * cols : (5 + c) * cols, :] = lo
    ahead_fluid = sampled(pieces, ahead_hot, ahead_ids[2:3], cols)
    _, ahead_new, ahead_row = updated(ahead_now, ahead_ids[3:4] - 1, ahead_fluid, drag_t, settle_t, heat_t)
    ahead_new = jnp.where(ahead_ids[3:4] > 0, ahead_new, 0.0)
    for d in range(5, 8):
        dx, dy = STEPS[d]
        span = slice((d - 5) * capacity, (d - 4) * capacity)
        filled, row = ahead_ids[3:4, span] > 0, ahead_row[:, span]
        shift = jnp.where(row == 0, float(dx * si), jnp.where(row == 1, float(dy * sj), 0.0))
        sending[d] = jnp.where(filled, ahead_new[:, span] - shift, 0.0)
        if remote:
            send(grain_copy(d), STEPS[d], True)

    if remote:
        @pl.when(last)
        def _():
            pl.semaphore_wait(answer_sem, high)
        send(halo_copy(1), halo_steps[1], last)
    loads[9].wait()
    for side, row in enumerate((sj - 1, 0)):
        for c in range(comps):
            edge_y[side, c] = gas_v[c, :, row, :]
        if remote:
            send(halo_copy(2 + side), halo_steps[2 + side], jnp.logical_not(slow))

    for n in range(slots // BLOCK):
        span = slice(n * BLOCK, (n + 1) * BLOCK)
        block_hot = one_hot(levels, cell_v[:, span] & (levels - 1))
        hot[:, span] = block_hot
        block_fluid = sampled(pieces, block_hot, cell_v[:, span] // levels, cols)
        for c in range(4):
            fluid[c : c + 1, span] = block_fluid[c]

    after, new, row = updated(now, kinds, [fluid[c : c + 1, :] for c in range(4)], drag_t, settle_t, heat_t)
    force = now[7:8] * (now - after)
    kept_v[...] = jnp.where(dests == 0, new, 0.0)
    first = jnp.where(dests <= 3, -1.0, 0.0)
    second = jnp.where((dests == 1) | (dests == 4), -1.0, jnp.where((dests == 3) | (dests == 5), 1.0, 0.0))
    sent = new - jnp.where(row == 0, first * si, jnp.where(row == 1, second * sj, 0.0))

    left = jnp.concatenate(
        [jnp.where(dests == d, s, 0.0) for s in split3(sent) for d in range(1, 6)] + [jnp.zeros((8, slots), F32)], axis=0
    ).astype(BF16)
    packed = lax.dot_general(left, slot_hot, NT, preferred_element_type=F32)
    packed = packed[:40] + packed[40:80] + packed[80:120]
    for d in range(5):
        sending[d] = packed[8 * d : 8 * (d + 1)]
        if remote:
            send(grain_copy(d), STEPS[d], late if d < 3 else True)
    if remote:
        for n in (2, 3):
            send(halo_copy(n), halo_steps[n], slow)

    f0 = force.astype(BF16).astype(F32)
    mask = lax.broadcasted_iota(I32, (cols, slots), 0) == column
    for k, f in enumerate((f0, force - f0)):
        for c in range(4):
            weighted[(4 * k + c) * cols : (4 * k + c + 1) * cols, :] = jnp.where(mask, f[3 + c : 4 + c], 0.0).astype(BF16)

    loads[10].wait()
    wide = CHUNK + 256
    for n in range(levels // CHUNK):
        lo, hi = n * CHUNK, (n + 1) * CHUNK
        dep = lax.dot_general(weighted[...], hot[lo:hi, :], NT, preferred_element_type=F32)
        dep = (dep[: 4 * cols] + dep[4 * cols :]).reshape(4, si, sj, CHUNK)
        jrow = lax.broadcasted_iota(I32, (sj, CHUNK), 0)
        zeros = jnp.zeros((sj, 128), F32)
        for c in range(comps):
            for i in range(si):
                here = gas_v[c, i, :, lo:hi]
                beside = jnp.where(jrow == 0, 0.0, pltpu.roll(here, 1, 0))
                beside = beside + jnp.where(jrow == sj - 1, 0.0, pltpu.roll(here, sj - 1, 0))
                if i > 0:
                    beside = beside + gas_v[c, i - 1, :, lo:hi]
                if i < si - 1:
                    beside = beside + gas_v[c, i + 1, :, lo:hi]
                below = gas_v[c, i, :, lo - 128 : lo] if lo > 0 else zeros
                above = gas_v[c, i, :, hi : hi + 128] if hi < levels else zeros
                full = jnp.concatenate([below, here, above], axis=1)
                beside = beside + pltpu.roll(full, 1, 1)[:, 128 : 128 + CHUNK]
                beside = beside + pltpu.roll(full, wide - 1, 1)[:, 128 : 128 + CHUNK]
                value = here + mix_v[i, :, lo:hi] * (beside - 6.0 * here)
                if c < 4:
                    value = value + dep[c, i]
                out_v[c, i, :, lo:hi] = value

    if not remote:
        landing[...] = sending[...]
        return

    for n in (1, 0, 2):
        @pl.when(early & inside((-1, -STEPS[5 + n][1])))
        def _():
            pl.semaphore_wait(reply_sem.at[n], 1)
        d = 2 - n
        if n == 1:
            send(halo_copy(1), halo_steps[1], early)
        send(grain_copy(d), STEPS[d], early)

    def back(step):
        return (-step[0], -step[1])

    for n in (2, 3):
        @pl.when(inside(back(halo_steps[n])))
        def _():
            halo_copy(n).wait_recv()
            j = (0, sj - 1)[n - 2]
            for c in range(comps):
                for i in range(si):
                    out_v[c, i, j : j + 1, :] = (
                        out_v[c, i, j : j + 1, :] + mix_v[i, j : j + 1, :] * halo_y[n - 2, c, i : i + 1, :]
                    )
    for n in (1, 0):
        @pl.when(inside(back(halo_steps[n])))
        def _():
            halo_copy(n).wait_recv()
            i = (0, si - 1)[n]
            for c in range(comps):
                out_v[c, i] = out_v[c, i] + mix_v[i] * halo_x[n, c]
    for d in range(8):
        came = inside(back(STEPS[d]))

        @pl.when(came)
        def _():
            grain_copy(d).wait_recv()

        @pl.when(jnp.logical_not(came))
        def _():
            landing[d] = jnp.zeros(landing.shape[1:], F32)
    for n in range(4):
        @pl.when(inside(halo_steps[n]))
        def _():
            halo_copy(n).wait_send()
    for d in range(8):
        @pl.when(inside(STEPS[d]))
        def _():
            grain_copy(d).wait_send()


def write_out(a, b, c, out_a, out_b, out_c, sems):
    copies = [
        pltpu.make_async_copy(src, dst, sems.at[n]) for n, (src, dst) in enumerate(((a, out_a), (b, out_b), (c, out_c)))
    ]
    for copy in copies:
        copy.start()
    for copy in copies:
        copy.wait()


def on_device(tiles, gas, mixing, grains, cell, kind, dest, slot, drag, settle, heat):
    comps, si, sj, levels = gas.shape
    attrs, slots = grains.shape
    capacity = slots // 16
    row = (1, slots)
    hbm = pl.BlockSpec(memory_space=pltpu.HBM)
    vmem = pl.BlockSpec(memory_space=pltpu.VMEM)
    held = (gas, mixing, grains, cell.reshape(row), kind.reshape(row), dest.reshape(row), slot.reshape(row), drag, settle, heat)
    held = tuple(pltpu.with_memory_space_constraint(x, pltpu.HBM) for x in held)
    results = pl.pallas_call(
        functools.partial(kernel, tiles),
        out_shape=(
            pltpu.VMEM(gas.shape, F32),
            pltpu.VMEM(grains.shape, F32),
            pltpu.VMEM((8, attrs, capacity), F32),
        ),
        in_specs=[hbm] * 10,
        out_specs=(vmem,) * 3,
        scratch_shapes=[
            pltpu.VMEM(gas.shape, F32),
            pltpu.VMEM(mixing.shape, F32),
            pltpu.VMEM(grains.shape, F32),
            pltpu.VMEM(row, I32),
            pltpu.VMEM(row, I32),
            pltpu.VMEM(row, I32),
            pltpu.VMEM(row, I32),
            pltpu.SMEM(drag.shape, F32),
            pltpu.SMEM(settle.shape, F32),
            pltpu.SMEM(heat.shape, F32),
            pltpu.VMEM((8 * si * sj, levels), BF16),
            pltpu.VMEM((levels, slots), BF16),
            pltpu.VMEM((8, slots), F32),
            pltpu.VMEM((8 * si * sj, slots), BF16),
            pltpu.VMEM((2, comps, si, levels), F32),
            pltpu.VMEM((2, comps, sj, levels), F32),
            pltpu.VMEM((2, comps, si, levels), F32),
            pltpu.VMEM((8, attrs, capacity), F32),
            pltpu.SemaphoreType.DMA((11,)),
            pltpu.SemaphoreType.DMA((12,)),
            pltpu.SemaphoreType.DMA((12,)),
            pltpu.SemaphoreType.REGULAR((3,)),
            pltpu.SemaphoreType.REGULAR,
        ],
        compiler_params=pltpu.CompilerParams(
            collective_id=0 if tiles[0] > 1 else None,
            has_side_effects=True,
            vmem_limit_bytes=40 * 1024 * 1024,
        ),
        name="ash_step",
    )(*held)
    shapes = tuple(jax.ShapeDtypeStruct(r.shape, F32) for r in results)
    results = tuple(pltpu.with_memory_space_constraint(r, pltpu.VMEM) for r in results)
    return pl.pallas_call(
        write_out,
        out_shape=shapes,
        in_specs=[vmem] * 3,
        out_specs=(hbm,) * 3,
        scratch_shapes=[pltpu.SemaphoreType.DMA((3,))],
        name="write_out",
    )(*results)


def solution(mesh):
    tiles = P(None, ("gx", "gy"))
    per_slot = P(("gx", "gy"))
    return jax.shard_map(
        functools.partial(on_device, (mesh.shape["gx"], mesh.shape["gy"])),
        mesh=mesh,
        in_specs=(P(None, "gx", "gy", None), P("gx", "gy", None), tiles) + (per_slot,) * 4 + (P(),) * 3,
        out_specs=(P(None, "gx", "gy", None), tiles, P(None, None, ("gx", "gy"))),
        check_vma=False,
    )
```

```python
import functools

import jax
import jax.numpy as jnp
from jax import lax
from jax.experimental import pallas as pl
from jax.experimental.pallas import tpu as pltpu
from jax.sharding import PartitionSpec as P

MESH = pl.DeviceIdType.MESH
STEPS = ((-1, -1), (-1, 0), (-1, 1), (0, -1), (0, 1), (1, -1), (1, 0), (1, 1))
F32, BF16, I32 = jnp.float32, jnp.bfloat16, jnp.int32
BLOCK = 256
CHUNK = 256
RUN = 16
FIRST = 3
NT = (((1,), (1,)), ((), ()))


def split2(x):
    hi = x.astype(BF16)
    return hi, (x - hi.astype(F32)).astype(BF16)


def split3(x):
    first = x.astype(BF16).astype(F32)
    second = (x - first).astype(BF16).astype(F32)
    return first, second, x - first - second


def one_hot(rows, ids):
    return jnp.where(lax.broadcasted_iota(I32, (rows, ids.shape[1]), 0) == ids, 1.0, 0.0).astype(BF16)


def sampled(pieces, hot, column, cols):
    picked = jnp.dot(pieces[...], hot, preferred_element_type=F32)
    picked = picked[: 4 * cols] + picked[4 * cols :]
    mask = lax.broadcasted_iota(I32, (cols, column.shape[1]), 0) == column
    return [
        jnp.sum(jnp.where(mask, picked[c * cols : (c + 1) * cols], 0.0), axis=0, keepdims=True) for c in range(4)
    ]


def updated(now, kinds, fluid, drag_t, settle_t, heat_t):
    drag = jnp.zeros(kinds.shape, F32)
    fall = jnp.zeros(kinds.shape, F32)
    heat = jnp.zeros(kinds.shape, F32)
    for k in range(drag_t.shape[0]):
        drag = jnp.where(kinds == k, drag_t[k], drag)
        fall = jnp.where(kinds == k, settle_t[k], fall)
        heat = jnp.where(kinds == k, heat_t[k], heat)
    row = lax.broadcasted_iota(I32, now.shape, 0)
    rate = jnp.where(row == 6, heat, drag)
    target = jnp.where(row == 6, fluid[3], fluid[2] - fall)
    target = jnp.where(row == 3, fluid[0], jnp.where(row == 4, fluid[1], target))
    after = (now + rate * target) / (1.0 + rate)
    moved = now + pltpu.roll(after, 5, 0)
    new = jnp.where(row < 3, moved, jnp.where(row == 7, now, after))
    return after, new, row


def kernel(
    tiles,
    gas, mixing, grains, cell, kind, dest, slot, drag_h, settle_h, heat_h,
    out_v, kept_v, landing,
    gas_v, mix_v, grain_v, cell_v, kind_v, dest_v, slot_v, drag_t, settle_t, heat_t,
    pieces, hot, fluid, weighted, edge_y, halo_x, halo_y, sending,
    load_sem, send_sem, recv_sem, reply_sem, answer_sem,
):
    comps, si, sj, levels = gas.shape
    cols = si * sj
    slots = grains.shape[1]
    capacity = landing.shape[2]
    nx, ny = tiles
    remote = nx > 1

    if remote:
        ix, iy = lax.axis_index("gx"), lax.axis_index("gy")
        place = lax.rem(ix, RUN)
        follows = ix < (nx // RUN - 1) * RUN
        early = (place == 0) & (ix > 0)
        late = jnp.logical_not(early)
        last = (place == RUN - 1) & follows
        usual = jnp.logical_not(last)
        slow = place >= RUN - 2

        def at(step):
            return (lax.rem(ix + step[0] + nx, nx), lax.rem(iy + step[1] + ny, ny))

        def inside(step):
            x, y = ix + step[0], iy + step[1]
            return (x >= 0) & (x < nx) & (y >= 0) & (y < ny)

        def number(flag):
            return flag.astype(I32)

        barrier = pltpu.get_barrier_semaphore()

        def greet(steps, when, semaphore):
            for n, step in enumerate(steps):
                @pl.when(when(step) & inside(step))
                def _():
                    pl.semaphore_signal(semaphore(n), inc=1, device_id=at(step), device_id_type=MESH)

        def first_round(step):
            target = place + step[0]
            return usual & (target >= 0) & (target < jnp.where(follows, RUN - 1, RUN)) | (early & (step[0] < 0))

        high = 1 + number(iy > 0) + number(iy < ny - 1)
        greet(STEPS, first_round, lambda n: barrier)

    def copy_of(n, src, dst, step):
        return pltpu.make_async_remote_copy(src, dst, send_sem.at[n], recv_sem.at[n], at(step), MESH)

    def halo_copy(n):
        if n == 0:
            return copy_of(0, gas.at[:FIRST, si - 1], halo_x.at[0, :FIRST], (1, 0))
        if n == 4:
            return copy_of(12, gas.at[FIRST:, si - 1], halo_x.at[0, FIRST:], (1, 0))
        if n == 1:
            return copy_of(1, gas.at[:, 0], halo_x.at[1], (-1, 0))
        return copy_of(n, edge_y.at[n - 2], halo_y.at[n - 2], ((0, 1), (0, -1))[n - 2])

    halo_steps = ((1, 0), (-1, 0), (0, 1), (0, -1), (1, 0))

    def grain_copy(d):
        return copy_of(4 + d, sending.at[d], landing.at[d], STEPS[d])

    def send(copy, step, when):
        @pl.when(when & inside(step))
        def _():
            copy.start()

    loads = [
        pltpu.make_async_copy(src, dst, load_sem.at[n])
        for n, (src, dst) in enumerate(
            (
                (grains, grain_v), (cell, cell_v), (kind, kind_v), (dest, dest_v), (slot, slot_v),
                (drag_h, drag_t), (settle_h, settle_t), (heat_h, heat_t),
                (gas.at[0:4], gas_v.at[0:4]), (gas.at[4:5], gas_v.at[4:5]), (mixing, mix_v),
            )
        )
    ]
    for load in loads:
        load.start()

    if remote:
        wide = 1 + number(place > 0) + number(place < RUN - 1)
        pl.semaphore_wait(barrier, jnp.where(last, high, wide * high - 1))
        send(halo_copy(0), halo_steps[0], True)
        greet(STEPS[5:], lambda step: last, lambda n: reply_sem.at[n])
        greet(STEPS[:3], lambda step: last, lambda n: barrier)
        greet(STEPS[5:], lambda step: (place == RUN - 2) & follows, lambda n: answer_sem)
        send(halo_copy(1), halo_steps[1], late & usual)

    for load in loads[:8]:
        load.wait()
    now, kinds, dests, cells = grain_v[...], kind_v[...], dest_v[...], cell_v[...]
    level, column = cells & (levels - 1), cells // levels
    slot_hot = one_hot(capacity, slot_v[...])
    ids = jnp.concatenate(
        [(level & -4), (level & 3), column, kinds + 1, jnp.zeros((4, slots), I32)], axis=0
    ).astype(F32)
    values = split3(now) + (ids,)
    left = jnp.concatenate(
        [jnp.where(dests == d, v, 0.0) for d in (6, 7, 8) for v in values], axis=0
    ).astype(BF16)
    ahead = lax.dot_general(left, slot_hot, NT, preferred_element_type=F32)
    parts = [ahead[32 * d : 32 * (d + 1)] for d in range(3)]
    groups = []
    for directions in ((7, 5), (6,)):
        part = jnp.concatenate([parts[d - 5] for d in directions], axis=1)
        ids = part[24:32].astype(I32)
        groups.append((directions, part[0:8] + part[8:16] + part[16:24], ids, one_hot(levels, ids[0:1] + ids[1:2])))
    loads[8].wait()
    for c in range(4):
        hi, lo = split2(gas_v[c].reshape(cols, levels))
        pieces[c * cols : (c + 1) * cols, :] = hi
        pieces[(4 + c) * cols : (5 + c) * cols, :] = lo
    for directions, ahead_now, ids, ahead_hot in groups:
        ahead_fluid = sampled(pieces, ahead_hot, ids[2:3], cols)
        _, ahead_new, row = updated(ahead_now, ids[3:4] - 1, ahead_fluid, drag_t, settle_t, heat_t)
        for n, d in enumerate(directions):
            dx, dy = STEPS[d]
            span = slice(n * capacity, (n + 1) * capacity)
            shift = jnp.where(row == 0, float(dx * si), jnp.where(row == 1, float(dy * sj), 0.0))
            sending[d] = jnp.where(ids[3:4] > 0, ahead_new - shift, 0.0)[:, span]
            if remote:
                send(grain_copy(d), STEPS[d], True)
    if remote:
        send(halo_copy(4), halo_steps[4], True)

    if remote:
        @pl.when(last)
        def _():
            pl.semaphore_wait(answer_sem, high)
        send(halo_copy(1), halo_steps[1], last)
    loads[9].wait()
    for side, row in enumerate((sj - 1, 0)):
        for c in range(comps):
            edge_y[side, c] = gas_v[c, :, row, :]
        if remote:
            send(halo_copy(2 + side), halo_steps[2 + side], jnp.logical_not(slow))

    for n in range(slots // BLOCK):
        span = slice(n * BLOCK, (n + 1) * BLOCK)
        block_hot = one_hot(levels, cell_v[:, span] & (levels - 1))
        hot[:, span] = block_hot
        block_fluid = sampled(pieces, block_hot, cell_v[:, span] // levels, cols)
        for c in range(4):
            fluid[c : c + 1, span] = block_fluid[c]

    after, new, row = updated(now, kinds, [fluid[c : c + 1, :] for c in range(4)], drag_t, settle_t, heat_t)
    force = now[7:8] * (now - after)
    kept_v[...] = jnp.where(dests == 0, new, 0.0)
    first = jnp.where(dests <= 3, -1.0, 0.0)
    second = jnp.where((dests == 1) | (dests == 4), -1.0, jnp.where((dests == 3) | (dests == 5), 1.0, 0.0))
    sent = new - jnp.where(row == 0, first * si, jnp.where(row == 1, second * sj, 0.0))

    left = jnp.concatenate(
        [jnp.where(dests == d, s, 0.0) for s in split3(sent) for d in range(1, 6)] + [jnp.zeros((8, slots), F32)], axis=0
    ).astype(BF16)
    packed = lax.dot_general(left, slot_hot, NT, preferred_element_type=F32)
    packed = packed[:40] + packed[40:80] + packed[80:120]
    for d in range(5):
        sending[d] = packed[8 * d : 8 * (d + 1)]
        if remote:
            send(grain_copy(d), STEPS[d], late if d < 3 else True)
    if remote:
        for n in (2, 3):
            send(halo_copy(n), halo_steps[n], slow)

    f0 = force.astype(BF16).astype(F32)
    mask = lax.broadcasted_iota(I32, (cols, slots), 0) == column
    for k, f in enumerate((f0, force - f0)):
        for c in range(4):
            weighted[(4 * k + c) * cols : (4 * k + c + 1) * cols, :] = jnp.where(mask, f[3 + c : 4 + c], 0.0).astype(BF16)

    loads[10].wait()
    wide = CHUNK + 256
    for n in range(levels // CHUNK):
        lo, hi = n * CHUNK, (n + 1) * CHUNK
        dep = lax.dot_general(weighted[...], hot[lo:hi, :], NT, preferred_element_type=F32)
        dep = (dep[: 4 * cols] + dep[4 * cols :]).reshape(4, si, sj, CHUNK)
        jrow = lax.broadcasted_iota(I32, (sj, CHUNK), 0)
        zeros = jnp.zeros((sj, 128), F32)
        for c in range(comps):
            for i in range(si):
                here = gas_v[c, i, :, lo:hi]
                beside = jnp.where(jrow == 0, 0.0, pltpu.roll(here, 1, 0))
                beside = beside + jnp.where(jrow == sj - 1, 0.0, pltpu.roll(here, sj - 1, 0))
                if i > 0:
                    beside = beside + gas_v[c, i - 1, :, lo:hi]
                if i < si - 1:
                    beside = beside + gas_v[c, i + 1, :, lo:hi]
                below = gas_v[c, i, :, lo - 128 : lo] if lo > 0 else zeros
                above = gas_v[c, i, :, hi : hi + 128] if hi < levels else zeros
                full = jnp.concatenate([below, here, above], axis=1)
                beside = beside + pltpu.roll(full, 1, 1)[:, 128 : 128 + CHUNK]
                beside = beside + pltpu.roll(full, wide - 1, 1)[:, 128 : 128 + CHUNK]
                value = here + mix_v[i, :, lo:hi] * (beside - 6.0 * here)
                if c < 4:
                    value = value + dep[c, i]
                out_v[c, i, :, lo:hi] = value

    if not remote:
        landing[...] = sending[...]
        return

    for n in (1, 0, 2):
        @pl.when(early & inside((-1, -STEPS[5 + n][1])))
        def _():
            pl.semaphore_wait(reply_sem.at[n], 1)
        d = 2 - n
        if n == 1:
            send(halo_copy(1), halo_steps[1], early)
        send(grain_copy(d), STEPS[d], early)

    def back(step):
        return (-step[0], -step[1])

    for n in (2, 3):
        @pl.when(inside(back(halo_steps[n])))
        def _():
            halo_copy(n).wait_recv()
            j = (0, sj - 1)[n - 2]
            for c in range(comps):
                for i in range(si):
                    out_v[c, i, j : j + 1, :] = (
                        out_v[c, i, j : j + 1, :] + mix_v[i, j : j + 1, :] * halo_y[n - 2, c, i : i + 1, :]
                    )
    def take_gx(n, among):
        @pl.when(inside(back(halo_steps[n])))
        def _():
            halo_copy(n).wait_recv()
            side = 1 if n == 1 else 0
            i = (0, si - 1)[side]
            for c in among:
                out_v[c, i] = out_v[c, i] + mix_v[i] * halo_x[side, c]

    def take_grains(d):
        came = inside(back(STEPS[d]))

        @pl.when(came)
        def _():
            grain_copy(d).wait_recv()

        @pl.when(jnp.logical_not(came))
        def _():
            landing[d] = jnp.zeros(landing.shape[1:], F32)

    take_gx(1, range(comps))
    for d in range(5):
        take_grains(d)
    for n in range(5):
        @pl.when(inside(halo_steps[n]))
        def _():
            halo_copy(n).wait_send()
    for d in range(8):
        @pl.when(inside(STEPS[d]))
        def _():
            grain_copy(d).wait_send()
    take_gx(0, range(FIRST))
    take_gx(4, range(FIRST, comps))
    for d in range(5, 8):
        take_grains(d)


def write_out(a, b, c, out_a, out_b, out_c, sems):
    copies = [
        pltpu.make_async_copy(src, dst, sems.at[n]) for n, (src, dst) in enumerate(((a, out_a), (b, out_b), (c, out_c)))
    ]
    for copy in copies:
        copy.start()
    for copy in copies:
        copy.wait()


def on_device(tiles, gas, mixing, grains, cell, kind, dest, slot, drag, settle, heat):
    comps, si, sj, levels = gas.shape
    attrs, slots = grains.shape
    capacity = slots // 16
    row = (1, slots)
    hbm = pl.BlockSpec(memory_space=pltpu.HBM)
    vmem = pl.BlockSpec(memory_space=pltpu.VMEM)
    held = (gas, mixing, grains, cell.reshape(row), kind.reshape(row), dest.reshape(row), slot.reshape(row), drag, settle, heat)
    held = tuple(pltpu.with_memory_space_constraint(x, pltpu.HBM) for x in held)
    results = pl.pallas_call(
        functools.partial(kernel, tiles),
        out_shape=(
            pltpu.VMEM(gas.shape, F32),
            pltpu.VMEM(grains.shape, F32),
            pltpu.VMEM((8, attrs, capacity), F32),
        ),
        in_specs=[hbm] * 10,
        out_specs=(vmem,) * 3,
        scratch_shapes=[
            pltpu.VMEM(gas.shape, F32),
            pltpu.VMEM(mixing.shape, F32),
            pltpu.VMEM(grains.shape, F32),
            pltpu.VMEM(row, I32),
            pltpu.VMEM(row, I32),
            pltpu.VMEM(row, I32),
            pltpu.VMEM(row, I32),
            pltpu.SMEM(drag.shape, F32),
            pltpu.SMEM(settle.shape, F32),
            pltpu.SMEM(heat.shape, F32),
            pltpu.VMEM((8 * si * sj, levels), BF16),
            pltpu.VMEM((levels, slots), BF16),
            pltpu.VMEM((8, slots), F32),
            pltpu.VMEM((8 * si * sj, slots), BF16),
            pltpu.VMEM((2, comps, si, levels), F32),
            pltpu.VMEM((2, comps, sj, levels), F32),
            pltpu.VMEM((2, comps, si, levels), F32),
            pltpu.VMEM((8, attrs, capacity), F32),
            pltpu.SemaphoreType.DMA((11,)),
            pltpu.SemaphoreType.DMA((13,)),
            pltpu.SemaphoreType.DMA((13,)),
            pltpu.SemaphoreType.REGULAR((3,)),
            pltpu.SemaphoreType.REGULAR,
        ],
        compiler_params=pltpu.CompilerParams(
            collective_id=0 if tiles[0] > 1 else None,
            has_side_effects=True,
            vmem_limit_bytes=40 * 1024 * 1024,
        ),
        name="ash_step",
    )(*held)
    shapes = tuple(jax.ShapeDtypeStruct(r.shape, F32) for r in results)
    results = tuple(pltpu.with_memory_space_constraint(r, pltpu.VMEM) for r in results)
    return pl.pallas_call(
        write_out,
        out_shape=shapes,
        in_specs=[vmem] * 3,
        out_specs=(hbm,) * 3,
        scratch_shapes=[pltpu.SemaphoreType.DMA((3,))],
        name="write_out",
    )(*results)


def solution(mesh):
    tiles = P(None, ("gx", "gy"))
    per_slot = P(("gx", "gy"))
    return jax.shard_map(
        functools.partial(on_device, (mesh.shape["gx"], mesh.shape["gy"])),
        mesh=mesh,
        in_specs=(P(None, "gx", "gy", None), P("gx", "gy", None), tiles) + (per_slot,) * 4 + (P(),) * 3,
        out_specs=(P(None, "gx", "gy", None), tiles, P(None, None, ("gx", "gy"))),
        check_vma=False,
    )
```

```python
import functools

import jax
import jax.numpy as jnp
from jax import lax
from jax.experimental import pallas as pl
from jax.experimental.pallas import tpu as pltpu
from jax.sharding import PartitionSpec as P

MESH = pl.DeviceIdType.MESH
STEPS = ((-1, -1), (-1, 0), (-1, 1), (0, -1), (0, 1), (1, -1), (1, 0), (1, 1))
F32, BF16, I32 = jnp.float32, jnp.bfloat16, jnp.int32
BLOCK = 256
CHUNK = 256
RUN = 16
AHEAD = {0: (0, 2), 4: (2, 3), 5: (3, 5)}
NT = (((1,), (1,)), ((), ()))


def split2(x):
    hi = x.astype(BF16)
    return hi, (x - hi.astype(F32)).astype(BF16)


def split3(x):
    first = x.astype(BF16).astype(F32)
    second = (x - first).astype(BF16).astype(F32)
    return first, second, x - first - second


def one_hot(rows, ids):
    return jnp.where(lax.broadcasted_iota(I32, (rows, ids.shape[1]), 0) == ids, 1.0, 0.0).astype(BF16)


def sampled(pieces, hot, column, cols):
    picked = jnp.dot(pieces[...], hot, preferred_element_type=F32)
    picked = picked[: 4 * cols] + picked[4 * cols :]
    mask = lax.broadcasted_iota(I32, (cols, column.shape[1]), 0) == column
    return [
        jnp.sum(jnp.where(mask, picked[c * cols : (c + 1) * cols], 0.0), axis=0, keepdims=True) for c in range(4)
    ]


def updated(now, kinds, fluid, drag_t, settle_t, heat_t):
    drag = jnp.zeros(kinds.shape, F32)
    fall = jnp.zeros(kinds.shape, F32)
    heat = jnp.zeros(kinds.shape, F32)
    for k in range(drag_t.shape[0]):
        drag = jnp.where(kinds == k, drag_t[k], drag)
        fall = jnp.where(kinds == k, settle_t[k], fall)
        heat = jnp.where(kinds == k, heat_t[k], heat)
    row = lax.broadcasted_iota(I32, now.shape, 0)
    rate = jnp.where(row == 6, heat, drag)
    target = jnp.where(row == 6, fluid[3], fluid[2] - fall)
    target = jnp.where(row == 3, fluid[0], jnp.where(row == 4, fluid[1], target))
    after = (now + rate * target) / (1.0 + rate)
    moved = now + pltpu.roll(after, 5, 0)
    new = jnp.where(row < 3, moved, jnp.where(row == 7, now, after))
    return after, new, row


def kernel(
    tiles,
    gas, mixing, grains, cell, kind, dest, slot, drag_h, settle_h, heat_h,
    out_v, kept_v, landing,
    gas_v, mix_v, grain_v, cell_v, kind_v, dest_v, slot_v, drag_t, settle_t, heat_t,
    pieces, hot, fluid, weighted, edge_y, halo_x, halo_y, sending,
    load_sem, send_sem, recv_sem, reply_sem, answer_sem,
):
    comps, si, sj, levels = gas.shape
    cols = si * sj
    slots = grains.shape[1]
    capacity = landing.shape[2]
    nx, ny = tiles
    remote = nx > 1

    loads = [
        pltpu.make_async_copy(src, dst, load_sem.at[n])
        for n, (src, dst) in enumerate(
            (
                (cell, cell_v), (dest, dest_v), (slot, slot_v), (kind, kind_v), (grains, grain_v),
                (gas.at[0:4], gas_v.at[0:4]), (drag_h, drag_t), (settle_h, settle_t), (heat_h, heat_t),
                (gas.at[4:5], gas_v.at[4:5]), (mixing, mix_v),
            )
        )
    ]
    for load in loads[:6]:
        load.start()

    if remote:
        ix, iy = lax.axis_index("gx"), lax.axis_index("gy")
        place = lax.rem(ix, RUN)
        follows = ix < (nx // RUN - 1) * RUN
        early = (place == 0) & (ix > 0)
        late = jnp.logical_not(early)
        last = (place == RUN - 1) & follows
        usual = jnp.logical_not(last)
        slow = place >= RUN - 2

        def at(step):
            return (lax.rem(ix + step[0] + nx, nx), lax.rem(iy + step[1] + ny, ny))

        def inside(step):
            x, y = ix + step[0], iy + step[1]
            return (x >= 0) & (x < nx) & (y >= 0) & (y < ny)

        def number(flag):
            return flag.astype(I32)

        barrier = pltpu.get_barrier_semaphore()

        def greet(steps, when, semaphore):
            for n, step in enumerate(steps):
                @pl.when(when(step) & inside(step))
                def _():
                    pl.semaphore_signal(semaphore(n), inc=1, device_id=at(step), device_id_type=MESH)

        def first_round(step):
            target = place + step[0]
            return usual & (target >= 0) & (target < jnp.where(follows, RUN - 1, RUN)) | (early & (step[0] < 0))

        high = 1 + number(iy > 0) + number(iy < ny - 1)
        greet(STEPS, first_round, lambda n: barrier)

    def copy_of(n, src, dst, step):
        return pltpu.make_async_remote_copy(src, dst, send_sem.at[n], recv_sem.at[n], at(step), MESH)

    def halo_copy(n):
        if n in (0, 4, 5):
            part = slice(*AHEAD[n])
            return copy_of(n if n == 0 else 8 + n, gas.at[part, si - 1], halo_x.at[0, part], (1, 0))
        if n == 1:
            return copy_of(1, gas.at[:, 0], halo_x.at[1], (-1, 0))
        return copy_of(n, edge_y.at[n - 2], halo_y.at[n - 2], ((0, 1), (0, -1))[n - 2])

    halo_steps = ((1, 0), (-1, 0), (0, 1), (0, -1), (1, 0), (1, 0))

    def grain_copy(d):
        return copy_of(4 + d, sending.at[d], landing.at[d], STEPS[d])

    def send(copy, step, when):
        @pl.when(when & inside(step))
        def _():
            copy.start()

    if remote:
        @pl.when(last)
        def _():
            pl.semaphore_wait(barrier, high)
            halo_copy(0).start()
    for load in loads[6:]:
        load.start()

    if remote:
        wide = 1 + number(place > 0) + number(place < RUN - 1)

        @pl.when(usual)
        def _():
            pl.semaphore_wait(barrier, wide * high - 1)
        send(halo_copy(0), halo_steps[0], usual)
        greet(STEPS[5:], lambda step: last, lambda n: reply_sem.at[n])
        greet(STEPS[:3], lambda step: last, lambda n: barrier)
        greet(STEPS[5:], lambda step: (place == RUN - 2) & follows, lambda n: answer_sem)
        send(halo_copy(1), halo_steps[1], late & usual)

    for load in loads[:5]:
        load.wait()
    now, kinds, dests, cells = grain_v[...], kind_v[...], dest_v[...], cell_v[...]
    level, column = cells & (levels - 1), cells // levels
    slot_hot = one_hot(capacity, slot_v[...])
    ids = jnp.concatenate(
        [(level & -4), (level & 3), column, kinds + 1, jnp.zeros((4, slots), I32)], axis=0
    ).astype(F32)
    values = split3(now) + (ids,)
    left = jnp.concatenate(
        [jnp.where(dests == d, v, 0.0) for d in (6, 7, 8) for v in values], axis=0
    ).astype(BF16)
    ahead = lax.dot_general(left, slot_hot, NT, preferred_element_type=F32)
    parts = [ahead[32 * d : 32 * (d + 1)] for d in range(3)]
    groups = []
    for directions in ((7,), (5, 6)):
        part = jnp.concatenate([parts[d - 5] for d in directions], axis=1)
        ids = part[24:32].astype(I32)
        groups.append((directions, part[0:8] + part[8:16] + part[16:24], ids, one_hot(levels, ids[0:1] + ids[1:2])))
    for load in loads[5:9]:
        load.wait()
    for c in range(4):
        hi, lo = split2(gas_v[c].reshape(cols, levels))
        pieces[c * cols : (c + 1) * cols, :] = hi
        pieces[(4 + c) * cols : (5 + c) * cols, :] = lo
    for directions, ahead_now, ids, ahead_hot in groups:
        ahead_fluid = sampled(pieces, ahead_hot, ids[2:3], cols)
        _, ahead_new, row = updated(ahead_now, ids[3:4] - 1, ahead_fluid, drag_t, settle_t, heat_t)
        for n, d in enumerate(directions):
            dx, dy = STEPS[d]
            span = slice(n * capacity, (n + 1) * capacity)
            shift = jnp.where(row == 0, float(dx * si), jnp.where(row == 1, float(dy * sj), 0.0))
            sending[d] = jnp.where(ids[3:4] > 0, ahead_new - shift, 0.0)[:, span]
            if remote:
                send(grain_copy(d), STEPS[d], True)
                if d > 5:
                    n = 4 if d == 7 else 5
                    send(halo_copy(n), halo_steps[n], True)

    if remote:
        @pl.when(last)
        def _():
            pl.semaphore_wait(answer_sem, high)
        send(halo_copy(1), halo_steps[1], last)
    loads[9].wait()
    for side, row in enumerate((sj - 1, 0)):
        for c in range(comps):
            edge_y[side, c] = gas_v[c, :, row, :]
        if remote:
            send(halo_copy(2 + side), halo_steps[2 + side], jnp.logical_not(slow))

    for n in range(slots // BLOCK):
        span = slice(n * BLOCK, (n + 1) * BLOCK)
        block_hot = one_hot(levels, cell_v[:, span] & (levels - 1))
        hot[:, span] = block_hot
        block_fluid = sampled(pieces, block_hot, cell_v[:, span] // levels, cols)
        for c in range(4):
            fluid[c : c + 1, span] = block_fluid[c]

    after, new, row = updated(now, kinds, [fluid[c : c + 1, :] for c in range(4)], drag_t, settle_t, heat_t)
    force = now[7:8] * (now - after)
    kept_v[...] = jnp.where(dests == 0, new, 0.0)
    first = jnp.where(dests <= 3, -1.0, 0.0)
    second = jnp.where((dests == 1) | (dests == 4), -1.0, jnp.where((dests == 3) | (dests == 5), 1.0, 0.0))
    sent = new - jnp.where(row == 0, first * si, jnp.where(row == 1, second * sj, 0.0))

    left = jnp.concatenate(
        [jnp.where(dests == d, s, 0.0) for s in split3(sent) for d in range(1, 6)] + [jnp.zeros((8, slots), F32)], axis=0
    ).astype(BF16)
    packed = lax.dot_general(left, slot_hot, NT, preferred_element_type=F32)
    packed = packed[:40] + packed[40:80] + packed[80:120]
    for d in range(5):
        sending[d] = packed[8 * d : 8 * (d + 1)]
        if remote:
            send(grain_copy(d), STEPS[d], late if d < 3 else True)
    if remote:
        for n in (2, 3):
            send(halo_copy(n), halo_steps[n], slow)

    f0 = force.astype(BF16).astype(F32)
    mask = lax.broadcasted_iota(I32, (cols, slots), 0) == column
    for k, f in enumerate((f0, force - f0)):
        for c in range(4):
            weighted[(4 * k + c) * cols : (4 * k + c + 1) * cols, :] = jnp.where(mask, f[3 + c : 4 + c], 0.0).astype(BF16)

    loads[10].wait()
    wide = CHUNK + 256
    for n in range(levels // CHUNK):
        lo, hi = n * CHUNK, (n + 1) * CHUNK
        dep = lax.dot_general(weighted[...], hot[lo:hi, :], NT, preferred_element_type=F32)
        dep = (dep[: 4 * cols] + dep[4 * cols :]).reshape(4, si, sj, CHUNK)
        jrow = lax.broadcasted_iota(I32, (sj, CHUNK), 0)
        zeros = jnp.zeros((sj, 128), F32)
        for c in range(comps):
            for i in range(si):
                here = gas_v[c, i, :, lo:hi]
                beside = jnp.where(jrow == 0, 0.0, pltpu.roll(here, 1, 0))
                beside = beside + jnp.where(jrow == sj - 1, 0.0, pltpu.roll(here, sj - 1, 0))
                if i > 0:
                    beside = beside + gas_v[c, i - 1, :, lo:hi]
                if i < si - 1:
                    beside = beside + gas_v[c, i + 1, :, lo:hi]
                below = gas_v[c, i, :, lo - 128 : lo] if lo > 0 else zeros
                above = gas_v[c, i, :, hi : hi + 128] if hi < levels else zeros
                full = jnp.concatenate([below, here, above], axis=1)
                beside = beside + pltpu.roll(full, 1, 1)[:, 128 : 128 + CHUNK]
                beside = beside + pltpu.roll(full, wide - 1, 1)[:, 128 : 128 + CHUNK]
                value = here + mix_v[i, :, lo:hi] * (beside - 6.0 * here)
                if c < 4:
                    value = value + dep[c, i]
                out_v[c, i, :, lo:hi] = value

    if not remote:
        landing[...] = sending[...]
        return

    for n in (1, 0, 2):
        @pl.when(early & inside((-1, -STEPS[5 + n][1])))
        def _():
            pl.semaphore_wait(reply_sem.at[n], 1)
        d = 2 - n
        if n == 1:
            send(halo_copy(1), halo_steps[1], early)
        send(grain_copy(d), STEPS[d], early)

    def back(step):
        return (-step[0], -step[1])

    for n in (2, 3):
        @pl.when(inside(back(halo_steps[n])))
        def _():
            halo_copy(n).wait_recv()
            j = (0, sj - 1)[n - 2]
            for c in range(comps):
                for i in range(si):
                    out_v[c, i, j : j + 1, :] = (
                        out_v[c, i, j : j + 1, :] + mix_v[i, j : j + 1, :] * halo_y[n - 2, c, i : i + 1, :]
                    )
    def take_gx(n, among):
        @pl.when(inside(back(halo_steps[n])))
        def _():
            halo_copy(n).wait_recv()
            side = 1 if n == 1 else 0
            i = (0, si - 1)[side]
            for c in among:
                out_v[c, i] = out_v[c, i] + mix_v[i] * halo_x[side, c]

    def take_grains(d):
        came = inside(back(STEPS[d]))

        @pl.when(came)
        def _():
            grain_copy(d).wait_recv()

        @pl.when(jnp.logical_not(came))
        def _():
            landing[d] = jnp.zeros(landing.shape[1:], F32)

    take_gx(1, range(comps))
    for d in range(5):
        take_grains(d)
    for n in range(6):
        @pl.when(inside(halo_steps[n]))
        def _():
            halo_copy(n).wait_send()
    for d in range(8):
        @pl.when(inside(STEPS[d]))
        def _():
            grain_copy(d).wait_send()
    for n in AHEAD:
        take_gx(n, range(*AHEAD[n]))
    for d in range(5, 8):
        take_grains(d)


def write_out(a, b, c, out_a, out_b, out_c, sems):
    copies = [
        pltpu.make_async_copy(src, dst, sems.at[n]) for n, (src, dst) in enumerate(((a, out_a), (b, out_b), (c, out_c)))
    ]
    for copy in copies:
        copy.start()
    for copy in copies:
        copy.wait()


def on_device(tiles, gas, mixing, grains, cell, kind, dest, slot, drag, settle, heat):
    comps, si, sj, levels = gas.shape
    attrs, slots = grains.shape
    capacity = slots // 16
    row = (1, slots)
    hbm = pl.BlockSpec(memory_space=pltpu.HBM)
    vmem = pl.BlockSpec(memory_space=pltpu.VMEM)
    held = (gas, mixing, grains, cell.reshape(row), kind.reshape(row), dest.reshape(row), slot.reshape(row), drag, settle, heat)
    held = tuple(pltpu.with_memory_space_constraint(x, pltpu.HBM) for x in held)
    results = pl.pallas_call(
        functools.partial(kernel, tiles),
        out_shape=(
            pltpu.VMEM(gas.shape, F32),
            pltpu.VMEM(grains.shape, F32),
            pltpu.VMEM((8, attrs, capacity), F32),
        ),
        in_specs=[hbm] * 10,
        out_specs=(vmem,) * 3,
        scratch_shapes=[
            pltpu.VMEM(gas.shape, F32),
            pltpu.VMEM(mixing.shape, F32),
            pltpu.VMEM(grains.shape, F32),
            pltpu.VMEM(row, I32),
            pltpu.VMEM(row, I32),
            pltpu.VMEM(row, I32),
            pltpu.VMEM(row, I32),
            pltpu.SMEM(drag.shape, F32),
            pltpu.SMEM(settle.shape, F32),
            pltpu.SMEM(heat.shape, F32),
            pltpu.VMEM((8 * si * sj, levels), BF16),
            pltpu.VMEM((levels, slots), BF16),
            pltpu.VMEM((8, slots), F32),
            pltpu.VMEM((8 * si * sj, slots), BF16),
            pltpu.VMEM((2, comps, si, levels), F32),
            pltpu.VMEM((2, comps, sj, levels), F32),
            pltpu.VMEM((2, comps, si, levels), F32),
            pltpu.VMEM((8, attrs, capacity), F32),
            pltpu.SemaphoreType.DMA((11,)),
            pltpu.SemaphoreType.DMA((14,)),
            pltpu.SemaphoreType.DMA((14,)),
            pltpu.SemaphoreType.REGULAR((3,)),
            pltpu.SemaphoreType.REGULAR,
        ],
        compiler_params=pltpu.CompilerParams(
            collective_id=0 if tiles[0] > 1 else None,
            has_side_effects=True,
            vmem_limit_bytes=40 * 1024 * 1024,
        ),
        name="ash_step",
    )(*held)
    shapes = tuple(jax.ShapeDtypeStruct(r.shape, F32) for r in results)
    results = tuple(pltpu.with_memory_space_constraint(r, pltpu.VMEM) for r in results)
    return pl.pallas_call(
        write_out,
        out_shape=shapes,
        in_specs=[vmem] * 3,
        out_specs=(hbm,) * 3,
        scratch_shapes=[pltpu.SemaphoreType.DMA((3,))],
        name="write_out",
    )(*results)


def solution(mesh):
    tiles = P(None, ("gx", "gy"))
    per_slot = P(("gx", "gy"))
    return jax.shard_map(
        functools.partial(on_device, (mesh.shape["gx"], mesh.shape["gy"])),
        mesh=mesh,
        in_specs=(P(None, "gx", "gy", None), P("gx", "gy", None), tiles) + (per_slot,) * 4 + (P(),) * 3,
        out_specs=(P(None, "gx", "gy", None), tiles, P(None, None, ("gx", "gy"))),
        check_vma=False,
    )
```

```python
import functools

import jax
import jax.numpy as jnp
from jax import lax
from jax.experimental import pallas as pl
from jax.experimental.pallas import tpu as pltpu
from jax.sharding import PartitionSpec as P

MESH = pl.DeviceIdType.MESH
STEPS = ((-1, -1), (-1, 0), (-1, 1), (0, -1), (0, 1), (1, -1), (1, 0), (1, 1))
F32, BF16, I32 = jnp.float32, jnp.bfloat16, jnp.int32
BLOCK = 256
CHUNK = 256
RUN = 16
AHEAD = {0: (0, 2), 4: (2, 3), 5: (3, 5)}
NT = (((1,), (1,)), ((), ()))


def split2(x):
    hi = x.astype(BF16)
    return hi, (x - hi.astype(F32)).astype(BF16)


def split3(x):
    first = x.astype(BF16).astype(F32)
    second = (x - first).astype(BF16).astype(F32)
    return first, second, x - first - second


def one_hot(rows, ids):
    return jnp.where(lax.broadcasted_iota(I32, (rows, ids.shape[1]), 0) == ids, 1.0, 0.0).astype(BF16)


def sampled(pieces, hot, column, cols):
    picked = jnp.dot(pieces[...], hot, preferred_element_type=F32)
    picked = picked[: 4 * cols] + picked[4 * cols :]
    mask = lax.broadcasted_iota(I32, (cols, column.shape[1]), 0) == column
    return [
        jnp.sum(jnp.where(mask, picked[c * cols : (c + 1) * cols], 0.0), axis=0, keepdims=True) for c in range(4)
    ]


def updated(now, kinds, fluid, drag_t, settle_t, heat_t):
    drag = jnp.zeros(kinds.shape, F32)
    fall = jnp.zeros(kinds.shape, F32)
    heat = jnp.zeros(kinds.shape, F32)
    for k in range(drag_t.shape[0]):
        drag = jnp.where(kinds == k, drag_t[k], drag)
        fall = jnp.where(kinds == k, settle_t[k], fall)
        heat = jnp.where(kinds == k, heat_t[k], heat)
    row = lax.broadcasted_iota(I32, now.shape, 0)
    rate = jnp.where(row == 6, heat, drag)
    target = jnp.where(row == 6, fluid[3], fluid[2] - fall)
    target = jnp.where(row == 3, fluid[0], jnp.where(row == 4, fluid[1], target))
    after = (now + rate * target) / (1.0 + rate)
    moved = now + pltpu.roll(after, 5, 0)
    new = jnp.where(row < 3, moved, jnp.where(row == 7, now, after))
    return after, new, row


def kernel(
    tiles,
    gas, mixing, grains, cell, kind, dest, slot, drag_h, settle_h, heat_h,
    out_v, kept_v, landing,
    gas_v, mix_v, grain_v, cell_v, kind_v, dest_v, slot_v, drag_t, settle_t, heat_t,
    pieces, hot, fluid, weighted, edge_y, halo_x, halo_y, sending,
    load_sem, send_sem, recv_sem, reply_sem, answer_sem,
):
    comps, si, sj, levels = gas.shape
    cols = si * sj
    slots = grains.shape[1]
    capacity = landing.shape[2]
    nx, ny = tiles
    remote = nx > 1

    loads = [
        pltpu.make_async_copy(src, dst, load_sem.at[n])
        for n, (src, dst) in enumerate(
            (
                (cell, cell_v), (dest, dest_v), (slot, slot_v), (kind, kind_v), (grains, grain_v),
                (gas.at[0:4], gas_v.at[0:4]), (drag_h, drag_t), (settle_h, settle_t), (heat_h, heat_t),
                (gas.at[4:5], gas_v.at[4:5]), (mixing, mix_v),
            )
        )
    ]
    for load in (loads[5], *loads[:5]):
        load.start()

    if remote:
        ix, iy = lax.axis_index("gx"), lax.axis_index("gy")
        place = lax.rem(ix, RUN)
        follows = ix < (nx // RUN - 1) * RUN
        early = (place == 0) & (ix > 0)
        late = jnp.logical_not(early)
        last = (place == RUN - 1) & follows
        usual = jnp.logical_not(last)
        slow = place >= RUN - 2

        def at(step):
            return (lax.rem(ix + step[0] + nx, nx), lax.rem(iy + step[1] + ny, ny))

        def inside(step):
            x, y = ix + step[0], iy + step[1]
            return (x >= 0) & (x < nx) & (y >= 0) & (y < ny)

        def number(flag):
            return flag.astype(I32)

        barrier = pltpu.get_barrier_semaphore()

        def greet(steps, when, semaphore):
            for n, step in enumerate(steps):
                @pl.when(when(step) & inside(step))
                def _():
                    pl.semaphore_signal(semaphore(n), inc=1, device_id=at(step), device_id_type=MESH)

        def first_round(step):
            target = place + step[0]
            return usual & (target >= 0) & (target < jnp.where(follows, RUN - 1, RUN)) | (early & (step[0] < 0))

        high = 1 + number(iy > 0) + number(iy < ny - 1)
        greet(STEPS, first_round, lambda n: barrier)

    def copy_of(n, src, dst, step):
        return pltpu.make_async_remote_copy(src, dst, send_sem.at[n], recv_sem.at[n], at(step), MESH)

    def halo_copy(n):
        if n in (0, 4, 5):
            part = slice(*AHEAD[n])
            return copy_of(n if n == 0 else 8 + n, gas.at[part, si - 1], halo_x.at[0, part], (1, 0))
        if n == 1:
            return copy_of(1, gas.at[:, 0], halo_x.at[1], (-1, 0))
        return copy_of(n, edge_y.at[n - 2], halo_y.at[n - 2], ((0, 1), (0, -1))[n - 2])

    halo_steps = ((1, 0), (-1, 0), (0, 1), (0, -1), (1, 0), (1, 0))

    def grain_copy(d):
        return copy_of(4 + d, sending.at[d], landing.at[d], STEPS[d])

    def send(copy, step, when):
        @pl.when(when & inside(step))
        def _():
            copy.start()

    if remote:
        @pl.when(last)
        def _():
            pl.semaphore_wait(barrier, high)
            halo_copy(0).start()
    for load in loads[6:]:
        load.start()

    if remote:
        wide = 1 + number(place > 0) + number(place < RUN - 1)

        @pl.when(usual)
        def _():
            pl.semaphore_wait(barrier, wide * high - 1)
        send(halo_copy(0), halo_steps[0], usual)
        greet(STEPS[5:], lambda step: last, lambda n: reply_sem.at[n])
        greet(STEPS[:3], lambda step: last, lambda n: barrier)
        greet(STEPS[5:], lambda step: (place == RUN - 2) & follows, lambda n: answer_sem)
        send(halo_copy(1), halo_steps[1], late & usual)

    for load in loads[:5]:
        load.wait()
    now, kinds, dests, cells = grain_v[...], kind_v[...], dest_v[...], cell_v[...]
    level, column = cells & (levels - 1), cells // levels
    slot_hot = one_hot(capacity, slot_v[...])
    ids = jnp.concatenate(
        [(level & -4), (level & 3), column, kinds + 1, jnp.zeros((4, slots), I32)], axis=0
    ).astype(F32)
    values = split3(now) + (ids,)
    left = jnp.concatenate(
        [jnp.where(dests == d, v, 0.0) for d in (6, 7, 8) for v in values], axis=0
    ).astype(BF16)
    ahead = lax.dot_general(left, slot_hot, NT, preferred_element_type=F32)
    parts = [ahead[32 * d : 32 * (d + 1)] for d in range(3)]
    groups = []
    for directions in ((7,), (5, 6)):
        part = jnp.concatenate([parts[d - 5] for d in directions], axis=1)
        ids = part[24:32].astype(I32)
        groups.append((directions, part[0:8] + part[8:16] + part[16:24], ids, one_hot(levels, ids[0:1] + ids[1:2])))
    for load in loads[5:9]:
        load.wait()
    for c in range(4):
        hi, lo = split2(gas_v[c].reshape(cols, levels))
        pieces[c * cols : (c + 1) * cols, :] = hi
        pieces[(4 + c) * cols : (5 + c) * cols, :] = lo
    for directions, ahead_now, ids, ahead_hot in groups:
        ahead_fluid = sampled(pieces, ahead_hot, ids[2:3], cols)
        _, ahead_new, row = updated(ahead_now, ids[3:4] - 1, ahead_fluid, drag_t, settle_t, heat_t)
        for n, d in enumerate(directions):
            dx, dy = STEPS[d]
            span = slice(n * capacity, (n + 1) * capacity)
            shift = jnp.where(row == 0, float(dx * si), jnp.where(row == 1, float(dy * sj), 0.0))
            sending[d] = jnp.where(ids[3:4] > 0, ahead_new - shift, 0.0)[:, span]
            if remote:
                send(grain_copy(d), STEPS[d], True)
                if d > 5:
                    n = 4 if d == 7 else 5
                    send(halo_copy(n), halo_steps[n], True)

    if remote:
        @pl.when(last)
        def _():
            pl.semaphore_wait(answer_sem, high)
        send(halo_copy(1), halo_steps[1], last)
    loads[9].wait()
    for side, row in enumerate((sj - 1, 0)):
        for c in range(comps):
            edge_y[side, c] = gas_v[c, :, row, :]
        if remote:
            send(halo_copy(2 + side), halo_steps[2 + side], jnp.logical_not(slow))

    for n in range(slots // BLOCK):
        span = slice(n * BLOCK, (n + 1) * BLOCK)
        block_hot = one_hot(levels, cell_v[:, span] & (levels - 1))
        hot[:, span] = block_hot
        block_fluid = sampled(pieces, block_hot, cell_v[:, span] // levels, cols)
        for c in range(4):
            fluid[c : c + 1, span] = block_fluid[c]

    after, new, row = updated(now, kinds, [fluid[c : c + 1, :] for c in range(4)], drag_t, settle_t, heat_t)
    force = now[7:8] * (now - after)
    kept_v[...] = jnp.where(dests == 0, new, 0.0)
    first = jnp.where(dests <= 3, -1.0, 0.0)
    second = jnp.where((dests == 1) | (dests == 4), -1.0, jnp.where((dests == 3) | (dests == 5), 1.0, 0.0))
    sent = new - jnp.where(row == 0, first * si, jnp.where(row == 1, second * sj, 0.0))

    left = jnp.concatenate(
        [jnp.where(dests == d, s, 0.0) for s in split3(sent) for d in range(1, 6)] + [jnp.zeros((8, slots), F32)], axis=0
    ).astype(BF16)
    packed = lax.dot_general(left, slot_hot, NT, preferred_element_type=F32)
    packed = packed[:40] + packed[40:80] + packed[80:120]
    for d in range(5):
        sending[d] = packed[8 * d : 8 * (d + 1)]
        if remote:
            send(grain_copy(d), STEPS[d], late if d < 3 else True)
    if remote:
        for n in (2, 3):
            send(halo_copy(n), halo_steps[n], slow)

    f0 = force.astype(BF16).astype(F32)
    mask = lax.broadcasted_iota(I32, (cols, slots), 0) == column
    for k, f in enumerate((f0, force - f0)):
        for c in range(4):
            weighted[(4 * k + c) * cols : (4 * k + c + 1) * cols, :] = jnp.where(mask, f[3 + c : 4 + c], 0.0).astype(BF16)

    loads[10].wait()
    wide = CHUNK + 256
    for n in range(levels // CHUNK):
        lo, hi = n * CHUNK, (n + 1) * CHUNK
        dep = lax.dot_general(weighted[...], hot[lo:hi, :], NT, preferred_element_type=F32)
        dep = (dep[: 4 * cols] + dep[4 * cols :]).reshape(4, si, sj, CHUNK)
        jrow = lax.broadcasted_iota(I32, (sj, CHUNK), 0)
        zeros = jnp.zeros((sj, 128), F32)
        for c in range(comps):
            for i in range(si):
                here = gas_v[c, i, :, lo:hi]
                beside = jnp.where(jrow == 0, 0.0, pltpu.roll(here, 1, 0))
                beside = beside + jnp.where(jrow == sj - 1, 0.0, pltpu.roll(here, sj - 1, 0))
                if i > 0:
                    beside = beside + gas_v[c, i - 1, :, lo:hi]
                if i < si - 1:
                    beside = beside + gas_v[c, i + 1, :, lo:hi]
                below = gas_v[c, i, :, lo - 128 : lo] if lo > 0 else zeros
                above = gas_v[c, i, :, hi : hi + 128] if hi < levels else zeros
                full = jnp.concatenate([below, here, above], axis=1)
                beside = beside + pltpu.roll(full, 1, 1)[:, 128 : 128 + CHUNK]
                beside = beside + pltpu.roll(full, wide - 1, 1)[:, 128 : 128 + CHUNK]
                value = here + mix_v[i, :, lo:hi] * (beside - 6.0 * here)
                if c < 4:
                    value = value + dep[c, i]
                out_v[c, i, :, lo:hi] = value

    if not remote:
        landing[...] = sending[...]
        return

    for n in (1, 0, 2):
        @pl.when(early & inside((-1, -STEPS[5 + n][1])))
        def _():
            pl.semaphore_wait(reply_sem.at[n], 1)
        d = 2 - n
        if n == 1:
            send(halo_copy(1), halo_steps[1], early)
        send(grain_copy(d), STEPS[d], early)

    def back(step):
        return (-step[0], -step[1])

    for n in (2, 3):
        @pl.when(inside(back(halo_steps[n])))
        def _():
            halo_copy(n).wait_recv()
            j = (0, sj - 1)[n - 2]
            for c in range(comps):
                for i in range(si):
                    out_v[c, i, j : j + 1, :] = (
                        out_v[c, i, j : j + 1, :] + mix_v[i, j : j + 1, :] * halo_y[n - 2, c, i : i + 1, :]
                    )
    def take_gx(n, among):
        @pl.when(inside(back(halo_steps[n])))
        def _():
            halo_copy(n).wait_recv()
            side = 1 if n == 1 else 0
            i = (0, si - 1)[side]
            for c in among:
                out_v[c, i] = out_v[c, i] + mix_v[i] * halo_x[side, c]

    def take_grains(d):
        came = inside(back(STEPS[d]))

        @pl.when(came)
        def _():
            grain_copy(d).wait_recv()

        @pl.when(jnp.logical_not(came))
        def _():
            landing[d] = jnp.zeros(landing.shape[1:], F32)

    take_gx(1, range(comps))
    for d in range(5):
        take_grains(d)
    for n in range(6):
        @pl.when(inside(halo_steps[n]))
        def _():
            halo_copy(n).wait_send()
    for d in range(8):
        @pl.when(inside(STEPS[d]))
        def _():
            grain_copy(d).wait_send()
    for n in AHEAD:
        take_gx(n, range(*AHEAD[n]))
    for d in range(5, 8):
        take_grains(d)


def write_out(a, b, c, out_a, out_b, out_c, sems):
    copies = [
        pltpu.make_async_copy(src, dst, sems.at[n]) for n, (src, dst) in enumerate(((a, out_a), (b, out_b), (c, out_c)))
    ]
    for copy in copies:
        copy.start()
    for copy in copies:
        copy.wait()


def on_device(tiles, gas, mixing, grains, cell, kind, dest, slot, drag, settle, heat):
    comps, si, sj, levels = gas.shape
    attrs, slots = grains.shape
    capacity = slots // 16
    row = (1, slots)
    hbm = pl.BlockSpec(memory_space=pltpu.HBM)
    vmem = pl.BlockSpec(memory_space=pltpu.VMEM)
    held = (gas, mixing, grains, cell.reshape(row), kind.reshape(row), dest.reshape(row), slot.reshape(row), drag, settle, heat)
    held = tuple(pltpu.with_memory_space_constraint(x, pltpu.HBM) for x in held)
    results = pl.pallas_call(
        functools.partial(kernel, tiles),
        out_shape=(
            pltpu.VMEM(gas.shape, F32),
            pltpu.VMEM(grains.shape, F32),
            pltpu.VMEM((8, attrs, capacity), F32),
        ),
        in_specs=[hbm] * 10,
        out_specs=(vmem,) * 3,
        scratch_shapes=[
            pltpu.VMEM(gas.shape, F32),
            pltpu.VMEM(mixing.shape, F32),
            pltpu.VMEM(grains.shape, F32),
            pltpu.VMEM(row, I32),
            pltpu.VMEM(row, I32),
            pltpu.VMEM(row, I32),
            pltpu.VMEM(row, I32),
            pltpu.SMEM(drag.shape, F32),
            pltpu.SMEM(settle.shape, F32),
            pltpu.SMEM(heat.shape, F32),
            pltpu.VMEM((8 * si * sj, levels), BF16),
            pltpu.VMEM((levels, slots), BF16),
            pltpu.VMEM((8, slots), F32),
            pltpu.VMEM((8 * si * sj, slots), BF16),
            pltpu.VMEM((2, comps, si, levels), F32),
            pltpu.VMEM((2, comps, sj, levels), F32),
            pltpu.VMEM((2, comps, si, levels), F32),
            pltpu.VMEM((8, attrs, capacity), F32),
            pltpu.SemaphoreType.DMA((11,)),
            pltpu.SemaphoreType.DMA((14,)),
            pltpu.SemaphoreType.DMA((14,)),
            pltpu.SemaphoreType.REGULAR((3,)),
            pltpu.SemaphoreType.REGULAR,
        ],
        compiler_params=pltpu.CompilerParams(
            collective_id=0 if tiles[0] > 1 else None,
            has_side_effects=True,
            vmem_limit_bytes=40 * 1024 * 1024,
        ),
        name="ash_step",
    )(*held)
    shapes = tuple(jax.ShapeDtypeStruct(r.shape, F32) for r in results)
    results = tuple(pltpu.with_memory_space_constraint(r, pltpu.VMEM) for r in results)
    return pl.pallas_call(
        write_out,
        out_shape=shapes,
        in_specs=[vmem] * 3,
        out_specs=(hbm,) * 3,
        scratch_shapes=[pltpu.SemaphoreType.DMA((3,))],
        name="write_out",
    )(*results)


def solution(mesh):
    tiles = P(None, ("gx", "gy"))
    per_slot = P(("gx", "gy"))
    return jax.shard_map(
        functools.partial(on_device, (mesh.shape["gx"], mesh.shape["gy"])),
        mesh=mesh,
        in_specs=(P(None, "gx", "gy", None), P("gx", "gy", None), tiles) + (per_slot,) * 4 + (P(),) * 3,
        out_specs=(P(None, "gx", "gy", None), tiles, P(None, None, ("gx", "gy"))),
        check_vma=False,
    )
```
